256 devices in a mesh: row: 8 (over x, core), col: 32 (over y, z).
Axes of the slice: x: 4, y: 4, z: 8, core: 2. Of those that a mesh axis runs over, the one named last changes fastest.
Arguments:
- queries: float32 [32, 131072], P(None, ('row', 'col'))
- block_spots: int32 [8, 32, 256], P('row', 'col'), may hold values from 0 to 4095, as said below
- live_blocks: int32 [8, 32], P('row', 'col'), may hold values from 1 to 256, as said below
- neighbor_cols: int32 [8, 32, 256, 16, 128], P('row', 'col'), may hold values from 0 to 127
- neighbor_sims: bfloat16 [8, 32, 256, 16, 128], P('row', 'col'), may hold values from 0.099609375 to 1
Outputs:
- solution: float32 [32, 131072], P(None, ('row', 'col'))
- residual: float32 [32, 131072], P(None, ('row', 'col'))
The draws below stay inside these ranges and needn't reach their ends.
Inputs may be any that keep to these rules, and one draw needn't show every extreme that they name: `block_spots`: within each index of the first two dimensions the 256 spots are distinct. `live_blocks`: some index of the array holds exactly 256.
All inputs are finite; a program needn't handle non-finite values.
Results may differ from the reference program's by a relative error of at most 0.01.
Values may be sent and summed in bfloat16 or wider, within the bound.
A program may use at most 128 MiB of HBM per device.

```python
import math
import jax
import jax.numpy as jnp
from jax import lax

Q = 32
SEG = 512
CAP = 256
KB = 16
ITERS = 2
NODES = 131072
N_ROW = 8
N_COL = 32


def draw_queries(key, part):
    key = jax.random.fold_in(key, 7)
    first_key, second_key, third_key = jax.random.split(key, 3)
    node_total = SEG * N_ROW * N_COL
    ramp = 1.0 + 2.0 * jnp.arange(node_total, dtype=jnp.float32) / (node_total - 1)
    row_scales = ramp * jnp.exp(jax.random.uniform(second_key, (node_total,), jnp.float32, 0.0, math.log(4.0)))
    col_scales = jnp.exp(jax.random.uniform(third_key, (Q, 1), jnp.float32, 0.0, math.log(2.0)))
    base_values = jax.random.normal(first_key, (Q, node_total), jnp.float32)
    return (0.25 * base_values * row_scales[None, :] * col_scales).astype(jnp.float32)


def pick_spots(device_key):
    per_seg = SEG // 128
    places = N_ROW * per_seg * N_COL * per_seg
    return jax.random.permutation(device_key, places)[:CAP]


def draw_block_spots(key, part):
    key = jax.random.fold_in(key, 11)
    device_keys = jax.random.split(key, N_ROW * N_COL)
    chosen = jax.vmap(pick_spots)(device_keys)
    return chosen.reshape(N_ROW, N_COL, CAP).astype(jnp.int32)


def draw_live_blocks(key, part):
    key = jax.random.fold_in(key, 12)
    count_key, busy_key = jax.random.split(key)
    counts = jax.random.randint(count_key, (N_ROW * N_COL,), CAP // 8, CAP // 2 + 1)
    busiest = jax.random.randint(busy_key, (), 0, N_ROW * N_COL)
    counts = jnp.where(jnp.arange(N_ROW * N_COL) == busiest, CAP, counts)
    return counts.reshape(N_ROW, N_COL).astype(jnp.int32)


def touch_ends(drawn, stream_key, low, high):
    dims = drawn.shape
    index_at = [jax.random.randint(jax.random.fold_in(stream_key, axis), (), 0, dims[axis]) for axis in range(len(dims))]
    drawn = drawn.at[tuple(index_at)].set(low)
    longest = dims.index(max(dims))
    index_at[longest] = (index_at[longest] + 1) % dims[longest]
    return drawn.at[tuple(index_at)].set(high)


def levels(key, shape, pieces, smallest, high):
    factor_of = 1.0
    for axis_at, parts in pieces:
        draws = jax.random.uniform(jax.random.fold_in(jax.random.fold_in(key, 6), axis_at), (parts,), jnp.float32, smallest / len(pieces), high / len(pieces))
        factor_of = factor_of * jnp.repeat(jnp.exp(draws), shape[axis_at] // parts).reshape((-1,) + (1,) * (len(shape) - 1 - axis_at))
    return factor_of


def setup_inputs(seed: int = 0) -> dict:
    splits = jax.random.split(jax.random.key(seed), 6)
    return {
        "queries": draw_queries(jax.random.fold_in(splits[5], 71), 0),
        "block_spots": draw_block_spots(jax.random.fold_in(splits[5], 71), 0),
        "live_blocks": draw_live_blocks(jax.random.fold_in(splits[5], 71), 0),
        "neighbor_cols": touch_ends(jax.random.randint(splits[3], (N_ROW, N_COL, CAP, KB, 128), 0, 128), jax.random.fold_in(splits[3], 1), 0, 127).astype(jnp.int32),
        "neighbor_sims": jnp.clip(jnp.exp(math.log(1.0) - 2.306499 * jax.random.uniform(splits[4], (N_ROW, N_COL, CAP, KB, 128), jnp.float32) ** levels(splits[4], (N_ROW, N_COL, CAP, KB, 128), ((0, 8), (1, 32)), -0.2, 0.2)), 0.099609375, 1.0).astype(jnp.bfloat16),
    }


graph_weight = 0.95

def fill_blocks(neighbor_idx, neighbor_val):
    lane_ids = jnp.arange(128, dtype=jnp.int32)
    running = jnp.zeros((neighbor_idx.shape[0], 128, 128), jnp.float32)
    for column_slot in range(neighbor_idx.shape[1]):
        matched = neighbor_idx[:, column_slot, :, None] == lane_ids
        running = running + jnp.where(matched, neighbor_val[:, column_slot, :, None].astype(jnp.float32), jnp.float32(0.0))
    return running.astype(jnp.bfloat16)

def spd_solve(matrix, right_side):
    factor = jnp.linalg.cholesky(matrix)
    partial_value = lax.linalg.triangular_solve(factor, right_side, left_side=True, lower=True)
    return lax.linalg.triangular_solve(factor, partial_value, left_side=True, lower=True, transpose_a=True)

def gram_matrix(first_rows, second_rows):
    return lax.dot_general(first_rows, second_rows, (((1,), (1,)), ((), ())), precision=lax.Precision.HIGHEST)

def symmetric(square):
    return 0.5 * (square + square.T)

def graph_product(vectors, block_spots, live_blocks, neighbor_cols, neighbor_sims):
    query_rows = vectors.shape[0]
    per_seg = SEG // 128
    col_span = N_COL * per_seg
    all_blocks = NODES // 128
    flattened = vectors.astype(jnp.float32).reshape(query_rows, all_blocks, 128)

    def device_step(totals, device):
        row_index = device // N_COL
        col_index = device % N_COL
        spot_list = block_spots[row_index, col_index]
        live_count = live_blocks[row_index, col_index]
        index_table = neighbor_cols[row_index, col_index]
        value_table = neighbor_sims[row_index, col_index]

        def group_turn(turn_index, partial_value):
            row_total, col_total = partial_value
            first_slot = turn_index * 16
            indices = lax.dynamic_slice_in_dim(index_table, first_slot, 16, 0)
            values = lax.dynamic_slice_in_dim(value_table, first_slot, 16, 0)
            placed = lax.dynamic_slice_in_dim(spot_list, first_slot, 16, 0)
            active = (first_slot + jnp.arange(16, dtype=jnp.int32) < live_count).astype(jnp.float32)
            blocks = fill_blocks(indices, values).astype(jnp.float32) * active[:, None, None]
            local_row = placed // col_span
            local_col = placed % col_span
            global_row = ((local_row // per_seg * N_COL + col_index) * per_seg + local_row % per_seg).astype(jnp.int32)
            global_col = ((row_index * N_COL + local_col // per_seg) * per_seg + local_col % per_seg).astype(jnp.int32)
            col_vecs = jnp.take(flattened, global_col, axis=1)
            row_vecs = jnp.take(flattened, global_row, axis=1)
            forward = jnp.einsum('sij,msj->msi', blocks, col_vecs, precision=lax.Precision.HIGHEST)
            backward = jnp.einsum('sij,msi->msj', blocks, row_vecs, precision=lax.Precision.HIGHEST)
            row_total = row_total.at[:, global_row].add(forward)
            col_total = col_total.at[:, global_col].add(backward)
            return (row_total, col_total)
        group_stop = ((live_count + 15) // 16).astype(jnp.int32)
        totals = lax.fori_loop(jnp.int32(0), group_stop, group_turn, totals)
        return (totals, None)
    zeroed = jnp.zeros((query_rows, all_blocks, 128), jnp.float32)
    (row_total, col_total), _ = lax.scan(device_step, (zeroed, zeroed), jnp.arange(N_ROW * N_COL, dtype=jnp.int32))
    return (0.5 * (row_total + col_total)).reshape(query_rows, NODES)

def reference(queries, block_spots, live_blocks, neighbor_cols, neighbor_sims):
    unit_vector = jnp.ones((1, NODES), jnp.bfloat16)
    degree = 1.0 + graph_product(unit_vector, block_spots, live_blocks, neighbor_cols, neighbor_sims)[0]
    scaling = 1.0 / jnp.sqrt(degree)

    def operator(vectors):
        scaled = (scaling * vectors).astype(jnp.bfloat16)
        return vectors - graph_weight * scaling * graph_product(scaled, block_spots, live_blocks, neighbor_cols, neighbor_sims)
    solution = jnp.zeros_like(queries)
    residual = queries
    direction = queries
    res_gram = symmetric(gram_matrix(residual, residual))
    for sweep_index in range(ITERS):
        applied = operator(direction)
        curvature = symmetric(gram_matrix(direction, applied))
        weights = spd_solve(curvature, res_gram)
        solution = solution + jnp.dot(weights.T, direction, precision=lax.Precision.HIGHEST)
        residual = residual - jnp.dot(weights.T, applied, precision=lax.Precision.HIGHEST)
        if sweep_index + 1 < ITERS:
            new_gram = symmetric(gram_matrix(residual, residual))
            mixing = spd_solve(res_gram, new_gram)
            direction = residual + jnp.dot(mixing.T, direction, precision=lax.Precision.HIGHEST)
            res_gram = new_gram
    return (solution, residual)
```

```python
import functools

import jax
import jax.numpy as jnp
from jax import lax
from jax.experimental import pallas as pl
from jax.experimental.pallas import tpu as pltpu
from jax.sharding import PartitionSpec as P

MESH = pl.DeviceIdType.MESH
HIGH = lax.Precision.HIGHEST
F32 = jnp.float32
BF16 = jnp.bfloat16
WEIGHT = 0.95
PS = 4
UNROLL = 8


def mm(first, second, transposed=False):
    dims = (((1,), (1 if transposed else 0,)), ((), ()))
    return lax.dot_general(first, second, dims, preferred_element_type=F32)


def mm_high(first, second, transposed=False):
    dims = (((1,), (1 if transposed else 0,)), ((), ()))
    return lax.dot_general(first, second, dims, precision=HIGH, preferred_element_type=F32)


def lanes(*parts):
    width = sum(p.shape[1] for p in parts)
    return jnp.concatenate(list(parts) + [jnp.zeros((parts[0].shape[0], 128 - width), F32)], axis=1)


def tall(small):
    return jnp.concatenate([small, jnp.zeros((128 - small.shape[0], 128), F32)], axis=0)


def flip(small):
    return tall(small).T[0:32]


def symmetric(small):
    return 0.5 * (small + flip(small))


def small_mm(first, second):
    return mm_high(first, tall(second))


def inverse(small):
    size = small.shape[0]
    row_ids = lax.broadcasted_iota(jnp.int32, small.shape, 0)
    lane_ids = lax.broadcasted_iota(jnp.int32, small.shape, 1)
    both = small + (row_ids + size == lane_ids).astype(F32)
    for k in range(size):
        pivot_row = both[k : k + 1, :] / both[k : k + 1, k : k + 1]
        both = jnp.where(row_ids == k, pivot_row, both - both[:, k : k + 1] * pivot_row)
    return lanes(both[:, size : 2 * size])


def kernel(
    sizes, q_ref, spots_ref, spot_row_ref, live_ref, cols_ref, sims_ref, sol_ref, res_ref,
    blocks, colsum, rowsum, basis, scale,
    xc, xr, xc2, xr2, fwd, bwd, out_r, out_c, out_rb, out_cb,
    deg_r, deg_c, deg_rr, deg_cr, scl_r, scl_c,
    yr, zs, zr, rr, gram, gram_in,
    ag_s, ag_r, ag_ys, ag_yr, dg_s, dg_r, sc_s, sc_r, rs_s, rs_r, rs_ys, rs_yr, ar_s, ar_r,
):
    R, Y, Z = sizes
    C = Y * Z
    RB, CB = R * PS, C * PS
    SLOTS = blocks.shape[0]
    shift = CB.bit_length() - 1
    a = lax.axis_index("row")
    b = lax.axis_index("col")
    y = b // Z
    z = b % Z

    def row_dev(k):
        return (lax.rem(a + k, R), b)

    def col_dev(k):
        return (a, lax.rem(b + k, C))

    def z_dev(k):
        return (a, y * Z + lax.rem(z + k, Z))

    def y_dev(k):
        return (a, lax.rem(y + k, Y) * Z + z)

    def copy(src, dst, ss, rs, dev):
        return pltpu.make_async_remote_copy(
            src_ref=src, dst_ref=dst, send_sem=ss, recv_sem=rs, device_id=dev, device_id_type=MESH
        )

    barrier = pltpu.get_barrier_semaphore()
    for k in range(1, R):
        pl.semaphore_signal(barrier, inc=1, device_id=row_dev(k), device_id_type=MESH)
    for k in range(1, C):
        pl.semaphore_signal(barrier, inc=1, device_id=col_dev(k), device_id_type=MESH)
    pl.semaphore_wait(barrier, R - 1 + C - 1)

    class Gather:
        def __init__(self, turn, col_buf, row_buf):
            mine_c = col_buf.at[pl.ds(b * PS, PS)]
            mine_r = row_buf.at[pl.ds(a * PS, PS)]
            self.row = [
                copy(mine_r, mine_r, ag_s.at[turn, k], ag_r.at[turn, k], row_dev(k)) for k in range(1, R)
            ]
            self.z = [
                copy(mine_c, mine_c, ag_s.at[turn, R + k], ag_r.at[turn, R + k], z_dev(k))
                for k in range(1, Z)
            ]
            self.y = []
            for kz in range(Z):
                chunk = col_buf.at[pl.ds((y * Z + lax.rem(z - kz + Z, Z)) * PS, PS)]
                self.y.append(
                    [
                        copy(chunk, chunk, ag_ys.at[turn, kz, ky], ag_yr.at[turn, kz, ky], y_dev(ky))
                        for ky in range(1, Y)
                    ]
                )

        def start(self):
            for c in self.y[0] + self.z + self.row:
                c.start()

        def forward(self):
            for kz in range(1, Z):
                self.z[kz - 1].wait_recv()
                for c in self.y[kz]:
                    c.start()

        def finish(self):
            for c in self.row:
                c.wait()
            for c in self.z:
                c.wait_send()
            for group in self.y:
                for c in group:
                    c.wait()

    basis[32:128, :] = jnp.zeros((96, PS * 128), F32)
    for p in range(PS):
        part = q_ref[:, p * 128 : (p + 1) * 128]
        basis[0:32, p * 128 : (p + 1) * 128] = part
        xc[b * PS + p] = part.astype(BF16)
        xr[a * PS + p] = part.astype(BF16)
    gather1 = Gather(0, xc, xr)
    gather1.start()

    lane_ids = lax.broadcasted_iota(jnp.int32, (128, 128), 0).astype(jnp.int16)
    ones = jnp.ones((8, 128), BF16)

    def build(s):
        idx = cols_ref[s]
        sim = sims_ref[s].astype(F32)
        value = jnp.zeros(sim.shape, F32)
        for t in range(idx.shape[0]):
            value = value + jnp.where(idx == idx[t : t + 1], sim[t : t + 1], 0.0)
        value = value.astype(BF16)
        idx = idx.astype(jnp.int16)
        block = jnp.zeros((128, 128), BF16)
        for t in range(idx.shape[0]):
            here = lane_ids == jnp.broadcast_to(idx[t : t + 1], (128, 128))
            block = jnp.where(here, jnp.broadcast_to(value[t : t + 1], (128, 128)), block)
        blocks[s] = block
        rowsum[pl.ds(s, 1), :] = jnp.sum(sim, axis=0, keepdims=True)
        colsum[pl.ds(s, 1), :] = mm(ones, block, True)[0:1]

    def build_range(low, high):
        def turn(g, carry):
            for u in range(UNROLL):
                build(g * UNROLL + u)
            return carry

        lax.fori_loop(low // UNROLL, high // UNROLL, turn, 0)

    build_range(0, SLOTS // 2)
    gather1.forward()
    build_range(SLOTS // 2, SLOTS)

    spot_row = spot_row_ref[...]
    live = live_ref[0, 0]
    used = lax.broadcasted_iota(jnp.int32, (1, SLOTS), 1) < live
    in_row = (lax.shift_right_logical(spot_row, shift) == lax.broadcasted_iota(jnp.int32, (RB, SLOTS), 0)) & used
    in_col = ((spot_row & (CB - 1)) == lax.broadcasted_iota(jnp.int32, (CB, SLOTS), 0)) & used
    in_row_f = jnp.where(in_row, 1.0, 0.0).astype(F32)
    in_col_f = jnp.where(in_col, 1.0, 0.0).astype(F32)
    row_degree = mm_high(in_row_f, rowsum[...])
    col_degree = mm_high(in_col_f, colsum[...])
    for g in range(R):
        deg_r[g] = row_degree[g * PS : (g + 1) * PS]
    for g in range(C):
        deg_c[g] = col_degree[g * PS : (g + 1) * PS]
    sends = []
    for k in range(1, C):
        sends.append(copy(deg_c.at[lax.rem(b + k, C)], deg_cr.at[k], dg_s.at[k], dg_r.at[k], col_dev(k)))
    for k in range(1, R):
        sends.append(
            copy(deg_r.at[lax.rem(a + k, R)], deg_rr.at[k], dg_s.at[C + k], dg_r.at[C + k], row_dev(k))
        )
    for c in sends:
        c.start()
    degree = deg_r[a] + deg_c[b]
    for c in sends:
        c.wait()
    for k in range(1, C):
        degree = degree + deg_cr[k]
    for k in range(1, R):
        degree = degree + deg_rr[k]
    degree = 1.0 + 0.5 * degree
    scaling = 1.0 / jnp.sqrt(degree)
    scl_r[a] = scaling
    scl_c[b] = scaling
    scale[...] = scaling
    sends = []
    for k in range(1, C):
        sends.append(copy(scl_c.at[b], scl_c.at[b], sc_s.at[k], sc_r.at[k], col_dev(k)))
    for k in range(1, R):
        sends.append(copy(scl_r.at[a], scl_r.at[a], sc_s.at[C + k], sc_r.at[C + k], row_dev(k)))
    for c in sends:
        c.start()
    gather1.finish()
    for c in sends:
        c.wait()

    def scale_part(buf, scl, g):
        factors = scl[g]
        for p in range(PS):
            buf[g * PS + p] = (buf[g * PS + p].astype(F32) * factors[p : p + 1]).astype(BF16)

    def scale_cols(g, carry):
        scale_part(xc, scl_c, g)
        return carry

    def scale_rows(g, carry):
        scale_part(xr, scl_r, g)
        return carry

    lax.fori_loop(0, C, scale_cols, 0)
    lax.fori_loop(0, R, scale_rows, 0)

    def apply(col_buf, row_buf):
        def pair(s):
            spot0, spot1 = spots_ref[s], spots_ref[s + 1]
            block0, block1 = blocks[s], blocks[s + 1]
            c0, c1 = col_buf[spot0 & (CB - 1)], col_buf[spot1 & (CB - 1)]
            r0 = row_buf[lax.shift_right_logical(spot0, shift)]
            r1 = row_buf[lax.shift_right_logical(spot1, shift)]
            ahead = mm(jnp.concatenate([c0, c1], 0), jnp.concatenate([block0, block1], 1))
            back = mm(jnp.concatenate([r0, r1], 0), jnp.concatenate([block0, block1], 0), True)
            fwd[:, s, :] = ahead[0:32, 0:128]
            fwd[:, s + 1, :] = ahead[32:64, 128:256]
            bwd[:, s, :] = back[0:32, 0:128]
            bwd[:, s + 1, :] = back[32:64, 128:256]

        def turn(g, carry):
            for u in range(UNROLL):
                pair(g * (2 * UNROLL) + 2 * u)
            return carry

        lax.fori_loop(0, SLOTS // (2 * UNROLL), turn, 0)
        pick_r = in_row_f.astype(BF16)
        pick_c = in_col_f.astype(BF16)

        def gather_sum(pick, terms):
            high = terms.astype(BF16)
            low = (terms - high.astype(F32)).astype(BF16)
            return mm(pick, high) + mm(pick, low)

        for m in range(32):
            out_c[:, m, :] = gather_sum(pick_c, bwd[m])
            out_r[:, m, :] = gather_sum(pick_r, fwd[m])

        def to_wire_c(v, carry):
            for p in range(PS):
                out_cb[v * PS + p] = out_c[v * PS + p].astype(BF16)
            return carry

        def to_wire_r(v, carry):
            for p in range(PS):
                out_rb[v * PS + p] = out_r[v * PS + p].astype(BF16)
            return carry

        lax.fori_loop(0, C, to_wire_c, 0)
        lax.fori_loop(0, R, to_wire_r, 0)

    def scatter_sum(turn):
        chunks = [(lax.rem(z + kz, Z)) for kz in range(Z)]
        ysends = []
        for kz in list(range(1, Z)) + [0]:
            group = []
            for ky in range(1, Y):
                src = out_cb.at[pl.ds((lax.rem(y + ky, Y) * Z + chunks[kz]) * PS, PS)]
                c = copy(
                    src, yr.at[turn, ky, kz], rs_ys.at[turn, ky, kz], rs_yr.at[turn, ky, kz], y_dev(ky)
                )
                c.start()
                group.append(c)
            ysends.append((kz, group))
        rsends = []
        for k in range(1, R):
            src = out_rb.at[pl.ds(lax.rem(a + k, R) * PS, PS)]
            c = copy(src, rr.at[turn, k], rs_s.at[turn, k], rs_r.at[turn, k], row_dev(k))
            c.start()
            rsends.append(c)
        zsends = []
        own = None
        for kz, group in ysends:
            for c in group:
                c.wait_recv()
            total = out_c[pl.ds((y * Z + chunks[kz]) * PS, PS)]
            for ky in range(1, Y):
                total = total + yr[turn, ky, kz].astype(F32)
            if kz:
                zs[turn, kz] = total.astype(BF16)
                c = copy(
                    zs.at[turn, kz], zr.at[turn, kz], rs_s.at[turn, R + kz], rs_r.at[turn, R + kz], z_dev(kz)
                )
                c.start()
                zsends.append(c)
            else:
                own = total
        own = own + out_r[pl.ds(a * PS, PS)]
        for k, c in enumerate(rsends):
            c.wait_recv()
            own = own + rr[turn, k + 1].astype(F32)
        for k, c in enumerate(zsends):
            c.wait_recv()
            own = own + zr[turn, k + 1].astype(F32)
        for kz, group in ysends:
            for c in group:
                c.wait_send()
        for c in rsends + zsends:
            c.wait_send()
        return own

    class Reduce:
        def __init__(self, turn):
            self.turn = turn

        def start(self, stage, value):
            turn = self.turn
            count, dev = ((R, row_dev), (Z, z_dev), (Y, y_dev))[stage]
            gram[turn, stage] = value
            self.value = value
            self.sends = []
            for k in range(1, count):
                c = copy(
                    gram.at[turn, stage],
                    gram_in.at[turn, stage, k],
                    ar_s.at[turn, stage, k],
                    ar_r.at[turn, stage, k],
                    dev(k),
                )
                c.start()
                self.sends.append(c)

        def finish(self, stage):
            total = self.value
            for k, c in enumerate(self.sends):
                c.wait()
                total = total + gram_in[self.turn, stage, k + 1]
            return total

    apply(xc, xr)
    summed = scatter_sum(0)
    scaling = scale[...]
    for p in range(PS):
        u1 = (0.5 * WEIGHT) * scaling[p : p + 1] * summed[p]
        basis[32:64, p * 128 : (p + 1) * 128] = u1
        part = (scaling[p : p + 1] * u1).astype(BF16)
        xc2[b * PS + p] = part
        xr2[a * PS + p] = part
    gather2 = Gather(1, xc2, xr2)
    gather2.start()
    early = Reduce(0)
    g0 = mm_high(basis[0:64, :], basis[...], True)
    early.start(0, lanes(g0[0:32, 0:64], g0[32:64, 32:64]))
    gather2.forward()
    early.start(1, early.finish(0))
    gather2.finish()
    early.start(2, early.finish(1))

    apply(xc2, xr2)
    grams = early.finish(2)
    summed = scatter_sum(1)
    scaling = scale[...]
    for p in range(PS):
        u2 = (0.5 * WEIGHT) * scaling[p : p + 1] * summed[p]
        basis[64:96, p * 128 : (p + 1) * 128] = u2
    late = Reduce(1)
    g2 = mm_high(basis[0:64, :], basis[...], True)
    late.start(0, lanes(g2[0:32, 64:96], g2[32:64, 64:96]))

    g00 = symmetric(lanes(grams[:, 0:32]))
    g01 = lanes(grams[:, 32:64])
    g11 = symmetric(lanes(grams[:, 64:96]))
    s01 = symmetric(g01)
    inv_curve = inverse(g00 - s01)
    inv_gram = inverse(g00)
    p1 = small_mm(g00, inv_curve)
    p0 = -small_mm(s01, inv_curve)
    p0_t, p1_t = flip(p0), flip(p1)
    newgram = small_mm(small_mm(p0, g00), p0_t) + small_mm(small_mm(p1, g11), p1_t)
    newgram = symmetric(newgram + 2.0 * small_mm(small_mm(p0, g01), p1_t))
    d0 = p0 + small_mm(newgram, inv_gram)
    e0, e1, e2 = d0, p1 - d0, -p1
    direction = lanes(d0[:, 0:32], p1[:, 0:32])
    applied = lanes(e0[:, 0:32], e1[:, 0:32], e2[:, 0:32])
    applied_t = tall(applied).T

    late.start(1, late.finish(0))
    late.start(2, late.finish(1))
    last = late.finish(2)
    whole = jnp.concatenate(
        [
            lanes(g00[:, 0:32], g01[:, 0:32], last[:, 0:32]),
            lanes(flip(g01)[:, 0:32], g11[:, 0:32], last[:, 32:64]),
        ],
        axis=0,
    )
    curve = symmetric(small_mm(direction, mm_high(whole, applied_t)))
    steps = small_mm(newgram, inverse(curve))
    sol_coef = lanes(p1[:, 0:32]) + small_mm(steps, direction)
    res_coef = lanes(p0[:, 0:32], p1[:, 0:32]) - small_mm(steps, applied)
    coef = jnp.concatenate([sol_coef, res_coef], axis=0)
    for p in range(PS):
        both = mm_high(coef, basis[:, p * 128 : (p + 1) * 128])
        sol_ref[:, p * 128 : (p + 1) * 128] = both[0:32]
        res_ref[:, p * 128 : (p + 1) * 128] = both[32:64]


def split_col(count):
    return (4, count // 4) if count >= 16 else (2, count // 2)


def solution(mesh):
    R, C = mesh.shape["row"], mesh.shape["col"]
    Y, Z = split_col(C)
    RB, CB = R * PS, C * PS

    def body(queries, block_spots, live_blocks, neighbor_cols, neighbor_sims):
        slots = block_spots.shape[2]
        vmem = pltpu.VMEM
        sems = pltpu.SemaphoreType.DMA
        scratch = [
            vmem((slots, 128, 128), BF16), vmem((slots, 128), F32), vmem((slots, 128), F32),
            vmem((128, PS * 128), F32), vmem((PS, 128), F32),
            vmem((CB, 32, 128), BF16), vmem((RB, 32, 128), BF16),
            vmem((CB, 32, 128), BF16), vmem((RB, 32, 128), BF16),
            vmem((32, slots, 128), F32), vmem((32, slots, 128), F32),
            vmem((RB, 32, 128), F32), vmem((CB, 32, 128), F32),
            vmem((RB, 32, 128), BF16), vmem((CB, 32, 128), BF16),
            vmem((R, PS, 128), F32), vmem((C, PS, 128), F32),
            vmem((R, PS, 128), F32), vmem((C, PS, 128), F32),
            vmem((R, PS, 128), F32), vmem((C, PS, 128), F32),
            vmem((2, Y, Z, PS, 32, 128), BF16), vmem((2, Z, PS, 32, 128), BF16),
            vmem((2, Z, PS, 32, 128), BF16), vmem((2, R, PS, 32, 128), BF16),
            vmem((2, 3, 32, 128), F32), vmem((2, 3, max(R, Z), 32, 128), F32),
            sems((2, R + Z)), sems((2, R + Z)), sems((2, Z, Y)), sems((2, Z, Y)),
            sems((C + R,)), sems((C + R,)), sems((C + R,)), sems((C + R,)),
            sems((2, R + Z)), sems((2, R + Z)), sems((2, Y, Z)), sems((2, Y, Z)),
            sems((2, 3, max(R, Z))), sems((2, 3, max(R, Z))),
        ]
        in_vmem = pl.BlockSpec(memory_space=pltpu.VMEM)
        in_smem = pl.BlockSpec(memory_space=pltpu.SMEM)
        shape = jax.ShapeDtypeStruct(queries.shape, F32)
        return pl.pallas_call(
            functools.partial(kernel, (R, Y, Z)),
            out_shape=(shape, shape),
            in_specs=[in_vmem, in_smem, in_vmem, in_smem, in_vmem, in_vmem],
            out_specs=(in_vmem, in_vmem),
            scratch_shapes=scratch,
            compiler_params=pltpu.CompilerParams(
                collective_id=0, has_side_effects=True, vmem_limit_bytes=52 * 1024 * 1024
            ),
        )(
            queries,
            block_spots[0, 0],
            block_spots[0],
            live_blocks,
            neighbor_cols[0, 0],
            neighbor_sims[0, 0],
        )

    placed = (
        P(None, ("row", "col")),
        P("row", "col", None),
        P("row", "col"),
        P("row", "col", None, None, None),
        P("row", "col", None, None, None),
    )
    return jax.shard_map(
        body,
        mesh=mesh,
        in_specs=placed,
        out_specs=(P(None, ("row", "col")), P(None, ("row", "col"))),
        check_vma=False,
    )
```

```python
import functools

import jax
import jax.numpy as jnp
from jax import lax
from jax.experimental import pallas as pl
from jax.experimental.pallas import tpu as pltpu
from jax.sharding import PartitionSpec as P

MESH = pl.DeviceIdType.MESH
HIGH = lax.Precision.HIGHEST
F32 = jnp.float32
BF16 = jnp.bfloat16
WEIGHT = 0.95
PS = 4
UNROLL = 8
BUILD = 16


def mm(first, second, transposed=False):
    dims = (((1,), (1 if transposed else 0,)), ((), ()))
    return lax.dot_general(first, second, dims, preferred_element_type=F32)


def mm_high(first, second, transposed=False):
    dims = (((1,), (1 if transposed else 0,)), ((), ()))
    return lax.dot_general(first, second, dims, precision=HIGH, preferred_element_type=F32)


def lanes(*parts):
    width = sum(p.shape[1] for p in parts)
    return jnp.concatenate(list(parts) + [jnp.zeros((parts[0].shape[0], 128 - width), F32)], axis=1)


def tall(small):
    return jnp.concatenate([small, jnp.zeros((128 - small.shape[0], small.shape[1]), F32)], axis=0)


def pack(square):
    return jnp.concatenate([square[8 * i : 8 * i + 8, 0:32] for i in range(4)], axis=1)


def unpack(packed):
    return lanes(jnp.concatenate([packed[:, 32 * i : 32 * i + 32] for i in range(4)], axis=0))


def wait_all(ref, sem):
    pltpu.make_async_copy(ref, ref, sem).wait()


def flip(small):
    return tall(small).T[0:32]


def symmetric(small):
    return 0.5 * (small + flip(small))


def small_mm(first, second):
    return mm_high(first, tall(second))


def inverse(small):
    size = small.shape[0]
    row_ids = lax.broadcasted_iota(jnp.int32, small.shape, 0)
    lane_ids = lax.broadcasted_iota(jnp.int32, small.shape, 1)
    both = small + (row_ids + size == lane_ids).astype(F32)
    for k in range(size):
        pivot_row = both[k : k + 1, :] / both[k : k + 1, k : k + 1]
        both = jnp.where(row_ids == k, pivot_row, both - both[:, k : k + 1] * pivot_row)
    return lanes(both[:, size : 2 * size])


def kernel(
    sizes, q_hbm, spots_ref, spot_row_hbm, live_ref, cols_hbm, sims_hbm, sol_ref, res_ref,
    q_ref, spot_row_ref, cols_ref, sims_ref, blocks, colsum, rowsum, basis, vectors, scale,
    xc, xr, xc2, xr2, fwd, bwd, out_r, out_c, out_rb, out_cb,
    deg_r, deg_c, deg_rr, deg_cr, scl_r, scl_c,
    yr, relay_in, relay_out, zs, zr, rr, gram_e, gram_ei, gram_l, gram_li,
    in_s, ag_z, ag_sem, dg_sem, sc_sem, rs_relay, rs_y, rs_sem, ar_sem,
):
    R, Y, Z = sizes
    C = Y * Z
    RB, CB = R * PS, C * PS
    SLOTS = blocks.shape[0]
    shift = CB.bit_length() - 1
    a = lax.axis_index("row")
    b = lax.axis_index("col")
    y = b // Z
    z = b % Z

    def row_dev(k):
        return (lax.rem(a + k, R), b)

    def col_dev(k):
        return (a, lax.rem(b + k, C))

    def z_dev(k):
        return (a, y * Z + lax.rem(z + k, Z))

    def y_dev(k):
        return (a, lax.rem(y + k, Y) * Z + z)

    def copy(src, dst, ss, rs, dev):
        return pltpu.make_async_remote_copy(
            src_ref=src, dst_ref=dst, send_sem=ss, recv_sem=rs, device_id=dev, device_id_type=MESH
        )

    barrier = pltpu.get_barrier_semaphore()
    for k in range(1, R):
        pl.semaphore_signal(barrier, inc=1, device_id=row_dev(k), device_id_type=MESH)
    for k in range(1, C):
        pl.semaphore_signal(barrier, inc=1, device_id=col_dev(k), device_id_type=MESH)

    quarter = SLOTS // 4
    loads = []
    for n in range(4):
        part = pl.ds(n * quarter, quarter)
        loads.append(
            (
                pltpu.make_async_copy(cols_hbm.at[part], cols_ref.at[part], in_s.at[n]),
                pltpu.make_async_copy(sims_hbm.at[part], sims_ref.at[part], in_s.at[4 + n]),
            )
        )
    others = (
        pltpu.make_async_copy(q_hbm, q_ref, in_s.at[8]),
        pltpu.make_async_copy(spot_row_hbm, spot_row_ref, in_s.at[9]),
    )
    for c in [*loads[0], *others, *loads[1], *loads[2], *loads[3]]:
        c.start()

    near_first = sorted(range(1, Z), key=lambda k: (min(k, Z - k), k))

    class Gather:
        def __init__(self, turn, col_buf, row_buf):
            self.turn, self.col_buf, self.row_buf = turn, col_buf, row_buf
            mine_c = col_buf.at[pl.ds(b * PS, PS)]
            mine_r = row_buf.at[pl.ds(a * PS, PS)]
            col_sent, row_sent, y_got, row_got = [ag_sem.at[turn, n] for n in range(4)]
            self.row = [copy(mine_r, mine_r, row_sent, row_got, row_dev(k)) for k in range(1, R)]
            self.z = {k: copy(mine_c, mine_c, col_sent, ag_z.at[turn, k], z_dev(k)) for k in range(1, Z)}
            self.y = {}
            for kz in range(Z):
                chunk = col_buf.at[pl.ds((y * Z + lax.rem(z - kz + Z, Z)) * PS, PS)]
                self.y[kz] = [
                    copy(chunk, chunk, col_sent, y_got, y_dev(ky)) for ky in ((2, 1, 3) if Y == 4 else (1,))
                ]

        def start(self):
            for c in self.y[0]:
                c.start()
            for kz in near_first:
                self.z[kz].start()
            for c in self.row:
                c.start()

        def forward(self):
            for kz in near_first:
                self.z[kz].wait_recv()
                for c in self.y[kz]:
                    c.start()

        def finish(self):
            col_sent, row_sent, y_got, row_got = [ag_sem.at[self.turn, n] for n in range(4)]
            wait_all(self.col_buf.at[pl.ds(0, (Y - 1) * Z * PS)], y_got)
            wait_all(self.row_buf.at[pl.ds(0, (R - 1) * PS)], row_got)
            wait_all(self.col_buf.at[pl.ds(0, (C - 1) * PS)], col_sent)
            wait_all(self.row_buf.at[pl.ds(0, (R - 1) * PS)], row_sent)

    gather1 = Gather(0, xc, xr)

    lane_ids = lax.broadcasted_iota(jnp.int32, (128, 128), 0).astype(jnp.int16)
    halves = (
        lax.broadcasted_iota(jnp.int32, (8, 256), 0)
        == lax.shift_right_logical(lax.broadcasted_iota(jnp.int32, (8, 256), 1), 7)
    )
    halves = jnp.where(halves, 1.0, 0.0).astype(BF16)

    def build(s):
        idx = cols_ref[s]
        sim = sims_ref[s].astype(F32)
        value = jnp.zeros(sim.shape, F32)
        for t in range(idx.shape[0]):
            value = value + jnp.where(idx == idx[t : t + 1], sim[t : t + 1], 0.0)
        value = value.astype(BF16)
        idx = idx.astype(jnp.int16)
        block = jnp.zeros((128, 128), BF16)
        for t in range(idx.shape[0]):
            here = lane_ids == jnp.broadcast_to(idx[t : t + 1], (128, 128))
            block = jnp.where(here, jnp.broadcast_to(value[t : t + 1], (128, 128)), block)
        blocks[s] = block
        rowsum[pl.ds(s, 1), :] = jnp.sum(sim, axis=0, keepdims=True)
        return block

    def build_turn(g, carry):
        turns = SLOTS // BUILD
        for n in range(4):

            @pl.when(g == n * turns // 4)
            def _():
                for c in loads[n]:
                    c.wait()

        @pl.when(g == turns * 7 // 16)
        def _():
            for c in others:
                c.wait()
            basis[32:128, :] = jnp.zeros((96, PS * 128), F32)
            for p in range(PS):
                part = q_ref[:, p * 128 : (p + 1) * 128]
                basis[0:32, p * 128 : (p + 1) * 128] = part
                xc[b * PS + p] = part.astype(BF16)
                xr[a * PS + p] = part.astype(BF16)
            pl.semaphore_wait(barrier, R - 1 + C - 1)
            gather1.start()

        @pl.when(g == turns * 12 // 16)
        def _():
            gather1.forward()

        for u in range(0, BUILD, 4):
            s = g * BUILD + u
            four = [build(s + v) for v in range(4)]
            pairs = jnp.concatenate(
                [jnp.concatenate([four[0], four[2]], 1), jnp.concatenate([four[1], four[3]], 1)], 0
            )
            sums = mm(halves, pairs, True)
            colsum[pl.ds(s, 1), :] = sums[0:1, 0:128]
            colsum[pl.ds(s + 1, 1), :] = sums[0:1, 128:256]
            colsum[pl.ds(s + 2, 1), :] = sums[1:2, 0:128]
            colsum[pl.ds(s + 3, 1), :] = sums[1:2, 128:256]
        return carry

    lax.fori_loop(0, SLOTS // BUILD, build_turn, 0)

    spot_row = spot_row_ref[...]
    live = live_ref[0, 0]
    used = lax.broadcasted_iota(jnp.int32, (1, SLOTS), 1) < live
    in_row = (lax.shift_right_logical(spot_row, shift) == lax.broadcasted_iota(jnp.int32, (RB, SLOTS), 0)) & used
    in_col = ((spot_row & (CB - 1)) == lax.broadcasted_iota(jnp.int32, (CB, SLOTS), 0)) & used
    in_row_f = jnp.where(in_row, 1.0, 0.0).astype(F32)
    in_col_f = jnp.where(in_col, 1.0, 0.0).astype(F32)
    row_degree = mm_high(in_row_f, rowsum[...])
    col_degree = mm_high(in_col_f, colsum[...])
    for g in range(R):
        deg_r[g] = row_degree[g * PS : (g + 1) * PS]
    for g in range(C):
        deg_c[g] = col_degree[g * PS : (g + 1) * PS]
    for k in range(1, C):
        copy(deg_c.at[lax.rem(b + k, C)], deg_cr.at[k], dg_sem.at[0], dg_sem.at[1], col_dev(k)).start()
    for k in range(1, R):
        copy(deg_r.at[lax.rem(a + k, R)], deg_rr.at[k], dg_sem.at[2], dg_sem.at[3], row_dev(k)).start()
    degree = deg_r[a] + deg_c[b]
    wait_all(deg_rr.at[pl.ds(1, R - 1)], dg_sem.at[3])
    wait_all(deg_cr.at[pl.ds(1, C - 1)], dg_sem.at[1])
    for k in range(1, C):
        degree = degree + deg_cr[k]
    for k in range(1, R):
        degree = degree + deg_rr[k]
    degree = 1.0 + 0.5 * degree
    scaling = 1.0 / jnp.sqrt(degree)
    scl_r[a] = scaling
    scl_c[b] = scaling
    scale[...] = scaling
    for k in range(1, C):
        copy(scl_c.at[b], scl_c.at[b], sc_sem.at[0], sc_sem.at[1], col_dev(k)).start()
    for k in range(1, R):
        copy(scl_r.at[a], scl_r.at[a], sc_sem.at[2], sc_sem.at[3], row_dev(k)).start()
    gather1.finish()
    wait_all(deg_rr.at[pl.ds(1, R - 1)], dg_sem.at[2])
    wait_all(deg_cr.at[pl.ds(1, C - 1)], dg_sem.at[0])
    for n in range(2):
        wait_all(scl_c.at[pl.ds(0, C - 1)], sc_sem.at[n])
        wait_all(scl_r.at[pl.ds(0, R - 1)], sc_sem.at[2 + n])

    def scale_part(buf, scl, g):
        factors = scl[g]
        for p in range(PS):
            buf[g * PS + p] = (buf[g * PS + p].astype(F32) * factors[p : p + 1]).astype(BF16)

    def scale_cols(g, carry):
        scale_part(xc, scl_c, g)
        return carry

    def scale_rows(g, carry):
        scale_part(xr, scl_r, g)
        return carry

    lax.fori_loop(0, C, scale_cols, 0)
    lax.fori_loop(0, R, scale_rows, 0)

    def apply(col_buf, row_buf):
        def pair(s):
            spot0, spot1 = spots_ref[s], spots_ref[s + 1]
            block0, block1 = blocks[s], blocks[s + 1]
            c0, c1 = col_buf[spot0 & (CB - 1)], col_buf[spot1 & (CB - 1)]
            r0 = row_buf[lax.shift_right_logical(spot0, shift)]
            r1 = row_buf[lax.shift_right_logical(spot1, shift)]
            ahead = mm(jnp.concatenate([c0, c1], 0), jnp.concatenate([block0, block1], 1))
            back = mm(jnp.concatenate([r0, r1], 0), jnp.concatenate([block0, block1], 0), True)
            fwd[:, s, :] = ahead[0:32, 0:128]
            fwd[:, s + 1, :] = ahead[32:64, 128:256]
            bwd[:, s, :] = back[0:32, 0:128]
            bwd[:, s + 1, :] = back[32:64, 128:256]

        def turn(g, carry):
            for u in range(UNROLL):
                pair(g * (2 * UNROLL) + 2 * u)
            return carry

        lax.fori_loop(0, SLOTS // (2 * UNROLL), turn, 0)
        pick_r = in_row_f.astype(BF16)
        pick_c = in_col_f.astype(BF16)

        def gather_sum(pick, terms):
            high = terms.astype(BF16)
            low = (terms - high.astype(F32)).astype(BF16)
            return mm(pick, high) + mm(pick, low)

        for m in range(32):
            out_c[:, m, :] = gather_sum(pick_c, bwd[m])

        def to_wire_c(v, carry):
            for p in range(2 * PS):
                out_cb[v * 2 * PS + p] = out_c[v * 2 * PS + p].astype(BF16)
            return carry

        lax.fori_loop(0, C // 2, to_wire_c, 0)

        def row_part():
            for m in range(32):
                out_r[:, m, :] = gather_sum(pick_r, fwd[m])
            for v in range(RB):
                out_rb[v] = out_r[v].astype(BF16)

        return row_part

    ways = (1, Y - 1) if Y == 4 else (1,)

    def relay_way(kz):
        return 0 if kz % 2 == 0 else 1

    def scatter_sum(turn, row_part, beside=None):
        places = [lax.rem(z + kz, Z) for kz in range(Z)]
        order = list(reversed(near_first)) + [0]
        y_sent, z_sent, z_got, row_sent, row_got = [rs_sem.at[turn, n] for n in range(5)]

        def part(ky, kz):
            return pl.ds((lax.rem(y + ky, Y) * Z + places[kz]) * PS, PS)

        def half(src, kz, w):
            copy(src, yr.at[turn, kz, w], y_sent, rs_y.at[turn, kz], y_dev(ways[w])).start()

        relays = {}
        if Y == 4:
            for kz in order:
                relays[kz] = copy(
                    out_cb.at[part(2, kz)],
                    relay_in.at[turn, kz],
                    y_sent,
                    rs_relay.at[turn, kz],
                    y_dev(ways[relay_way(kz)]),
                )
                relays[kz].start()
        for kz in order:
            for w, ky in enumerate(ways):
                if Y != 4 or w != relay_way(kz):
                    half(out_cb.at[part(ky, kz)], kz, w)
        row_part()
        for k in range(1, R):
            src = out_rb.at[pl.ds(lax.rem(a + k, R) * PS, PS)]
            copy(src, rr.at[turn, k], row_sent, row_got, row_dev(k)).start()
        result = beside() if beside else None
        if Y == 4:
            for kz in order:
                w = relay_way(kz)
                relays[kz].wait_recv()
                total = out_c[part(ways[w], kz)] + relay_in[turn, kz].astype(F32)
                relay_out[turn, kz] = total.astype(BF16)
                half(relay_out.at[turn, kz], kz, w)
        own = out_r[pl.ds(a * PS, PS)]
        for kz in order:
            total = out_c[part(0, kz)]
            wait_all(yr.at[turn, kz], rs_y.at[turn, kz])
            for w in range(len(ways)):
                total = total + yr[turn, kz, w].astype(F32)
            if kz:
                zs[turn, kz] = total.astype(BF16)
                copy(zs.at[turn, kz], zr.at[turn, kz], z_sent, z_got, z_dev(kz)).start()
            else:
                own = own + total
        wait_all(rr.at[turn, pl.ds(1, R - 1)], row_got)
        for k in range(1, R):
            own = own + rr[turn, k].astype(F32)
        wait_all(zr.at[turn, pl.ds(1, Z - 1)], z_got)
        for kz in range(1, Z):
            own = own + zr[turn, kz].astype(F32)
        wait_all(out_cb.at[pl.ds(0, (Y - 1) * Z * PS)], y_sent)
        wait_all(rr.at[turn, pl.ds(1, R - 1)], row_sent)
        wait_all(zr.at[turn, pl.ds(1, Z - 1)], z_sent)
        return own, result

    class Reduce:
        def __init__(self, turn, buf, buf_in):
            self.turn, self.buf, self.buf_in = turn, buf, buf_in

        def start(self, stage, value):
            count, dev = ((R, row_dev), (Z, z_dev), (Y, y_dev))[stage]
            self.buf[stage] = value
            for k in range(1, count):
                copy(
                    self.buf.at[stage],
                    self.buf_in.at[stage, k],
                    ar_sem.at[self.turn, stage, 0],
                    ar_sem.at[self.turn, stage, 1],
                    dev(k),
                ).start()

        def finish(self, stage):
            count = (R, Z, Y)[stage]
            there = self.buf_in.at[stage, pl.ds(1, count - 1)]
            wait_all(there, ar_sem.at[self.turn, stage, 1])
            total = self.buf[stage]
            for k in range(1, count):
                total = total + self.buf_in[stage, k]
            wait_all(there, ar_sem.at[self.turn, stage, 0])
            return total

    row_part = apply(xc, xr)
    summed, _ = scatter_sum(0, row_part)
    scaling = scale[...]
    for p in range(PS):
        u1 = (0.5 * WEIGHT) * scaling[p : p + 1] * summed[p]
        basis[32:64, p * 128 : (p + 1) * 128] = u1
        part = (scaling[p : p + 1] * u1).astype(BF16)
        xc2[b * PS + p] = part
        xr2[a * PS + p] = part
    gather2 = Gather(1, xc2, xr2)
    gather2.start()
    early = Reduce(0, gram_e, gram_ei)
    g0 = mm_high(basis[0:64, :], basis[0:64, :], True)
    early.start(
        0, jnp.concatenate([pack(g0[0:32]), pack(g0[0:32, 32:64]), pack(g0[32:64, 32:64])], axis=0)
    )
    gather2.forward()
    early.start(1, early.finish(0))
    gather2.finish()
    early.start(2, early.finish(1))

    def first_systems():
        grams = early.finish(2)
        g00 = symmetric(unpack(grams[0:8]))
        g01 = unpack(grams[8:16])
        g11 = symmetric(unpack(grams[16:24]))
        s01 = symmetric(g01)
        inv_curve = inverse(g00 - s01)
        inv_gram = inverse(g00)
        p1 = small_mm(g00, inv_curve)
        p0 = -small_mm(s01, inv_curve)
        p0_t, p1_t = flip(p0), flip(p1)
        newgram = small_mm(small_mm(p0, g00), p0_t) + small_mm(small_mm(p1, g11), p1_t)
        newgram = symmetric(newgram + 2.0 * small_mm(small_mm(p0, g01), p1_t))
        d0 = p0 + small_mm(newgram, inv_gram)
        direction = lanes(d0[:, 0:32], p1[:, 0:32])
        applied = lanes(d0[:, 0:32], p1[:, 0:32] - d0[:, 0:32], -p1[:, 0:32])
        whole = jnp.concatenate(
            [
                lanes(g00[:, 0:32], g01[:, 0:32], g11[:, 0:32]),
                lanes(flip(g01)[:, 0:32], g11[:, 0:32]),
            ],
            axis=0,
        )
        known = small_mm(direction, mm_high(whole, tall(applied).T))
        coef = jnp.concatenate([direction, lanes(p0[:, 0:32], p1[:, 0:32]), p1], axis=0)
        vectors[...] = mm_high(coef, basis[...])
        return newgram, p1, p1_t, applied, known

    row_part = apply(xc2, xr2)
    summed, small = scatter_sum(1, row_part, first_systems)
    newgram, p1, p1_t, applied, known = small
    scaling = scale[...]
    for p in range(PS):
        u2 = (0.5 * WEIGHT) * scaling[p : p + 1] * summed[p]
        basis[64:96, p * 128 : (p + 1) * 128] = u2
    late = Reduce(1, gram_l, gram_li)
    late.start(0, pack(mm_high(basis[32:64, :], basis[64:96, :], True)))
    image = mm_high(applied, basis[...])
    late.start(1, late.finish(0))
    late.start(2, late.finish(1))
    g12 = unpack(late.finish(2))
    curve = symmetric(known - small_mm(small_mm(p1, g12), p1_t))
    steps = small_mm(newgram, inverse(curve))
    sol_ref[...] = vectors[64:96, :] + mm_high(steps, tall(vectors[0:32, :]))
    res_ref[...] = vectors[32:64, :] - mm_high(steps, tall(image))


def split_col(count):
    return (4, count // 4) if count >= 8 else (2, count // 2)


def solution(mesh):
    R, C = mesh.shape["row"], mesh.shape["col"]
    Y, Z = split_col(C)
    RB, CB = R * PS, C * PS

    def body(queries, block_spots, live_blocks, neighbor_cols, neighbor_sims):
        slots = block_spots.shape[2]
        vmem = pltpu.VMEM
        sems = pltpu.SemaphoreType.DMA
        ways = 2 if Y == 4 else 1
        scratch = [
            vmem(queries.shape, F32), vmem((1, slots), jnp.int32),
            vmem(neighbor_cols.shape[2:], jnp.int32), vmem(neighbor_sims.shape[2:], BF16),
            vmem((slots, 128, 128), BF16), vmem((slots, 128), F32), vmem((slots, 128), F32),
            vmem((128, PS * 128), F32), vmem((96, PS * 128), F32), vmem((PS, 128), F32),
            vmem((CB, 32, 128), BF16), vmem((RB, 32, 128), BF16),
            vmem((CB, 32, 128), BF16), vmem((RB, 32, 128), BF16),
            vmem((32, slots, 128), F32), vmem((32, slots, 128), F32),
            vmem((RB, 32, 128), F32), vmem((CB, 32, 128), F32),
            vmem((RB, 32, 128), BF16), vmem((CB, 32, 128), BF16),
            vmem((R, PS, 128), F32), vmem((C, PS, 128), F32),
            vmem((R, PS, 128), F32), vmem((C, PS, 128), F32),
            vmem((R, PS, 128), F32), vmem((C, PS, 128), F32),
            vmem((2, Z, ways, PS, 32, 128), BF16), vmem((2, Z, PS, 32, 128), BF16),
            vmem((2, Z, PS, 32, 128), BF16), vmem((2, Z, PS, 32, 128), BF16),
            vmem((2, Z, PS, 32, 128), BF16), vmem((2, R, PS, 32, 128), BF16),
            vmem((3, 24, 128), F32), vmem((3, max(R, Z, Y), 24, 128), F32),
            vmem((3, 8, 128), F32), vmem((3, max(R, Z, Y), 8, 128), F32),
            sems((10,)), sems((2, Z)), sems((2, 4)), sems((4,)), sems((4,)),
            sems((2, Z)), sems((2, Z)), sems((2, 5)), sems((2, 3, 2)),
        ]
        in_vmem = pl.BlockSpec(memory_space=pltpu.VMEM)
        in_any = pl.BlockSpec(memory_space=pl.ANY)
        in_smem = pl.BlockSpec(memory_space=pltpu.SMEM)
        shape = jax.ShapeDtypeStruct(queries.shape, F32)
        return pl.pallas_call(
            functools.partial(kernel, (R, Y, Z)),
            out_shape=(shape, shape),
            in_specs=[in_any, in_smem, in_any, in_smem, in_any, in_any],
            out_specs=(in_vmem, in_vmem),
            scratch_shapes=scratch,
            compiler_params=pltpu.CompilerParams(
                collective_id=0, has_side_effects=True, vmem_limit_bytes=60 * 1024 * 1024
            ),
        )(
            queries,
            block_spots[0, 0],
            block_spots[0],
            live_blocks,
            neighbor_cols[0, 0],
            neighbor_sims[0, 0],
        )

    placed = (
        P(None, ("row", "col")),
        P("row", "col", None),
        P("row", "col"),
        P("row", "col", None, None, None),
        P("row", "col", None, None, None),
    )
    return jax.shard_map(
        body,
        mesh=mesh,
        in_specs=placed,
        out_specs=(P(None, ("row", "col")), P(None, ("row", "col"))),
        check_vma=False,
    )
```

```python
import functools

import jax
import jax.numpy as jnp
from jax import lax
from jax.experimental import pallas as pl
from jax.experimental.pallas import tpu as pltpu
from jax.sharding import PartitionSpec as P

MESH = pl.DeviceIdType.MESH
HIGH = lax.Precision.HIGHEST
F32 = jnp.float32
BF16 = jnp.bfloat16
WEIGHT = 0.95
PS = 4
UNROLL = 4
BUILD = 16


def mm(first, second, transposed=False):
    dims = (((1,), (1 if transposed else 0,)), ((), ()))
    return lax.dot_general(first, second, dims, preferred_element_type=F32)


def mm_high(first, second, transposed=False):
    dims = (((1,), (1 if transposed else 0,)), ((), ()))
    return lax.dot_general(first, second, dims, precision=HIGH, preferred_element_type=F32)


def lanes(*parts):
    width = sum(p.shape[1] for p in parts)
    return jnp.concatenate(list(parts) + [jnp.zeros((parts[0].shape[0], 128 - width), F32)], axis=1)


def tall(small):
    return jnp.concatenate([small, jnp.zeros((128 - small.shape[0], small.shape[1]), F32)], axis=0)


def pack(square):
    return jnp.concatenate([square[8 * i : 8 * i + 8, 0:32] for i in range(4)], axis=1)


def unpack(packed):
    return lanes(jnp.concatenate([packed[:, 32 * i : 32 * i + 32] for i in range(4)], axis=0))


def wait_all(ref, sem):
    pltpu.make_async_copy(ref, ref, sem).wait()


def flip(small):
    return tall(small).T[0:32]


def symmetric(small):
    return 0.5 * (small + flip(small))


def small_mm(first, second):
    return mm_high(first, tall(second))


def inverse(small):
    size = small.shape[0]
    row_ids = lax.broadcasted_iota(jnp.int32, small.shape, 0)
    lane_ids = lax.broadcasted_iota(jnp.int32, small.shape, 1)
    both = small + (row_ids + size == lane_ids).astype(F32)
    for k in range(size):
        pivot_row = both[k : k + 1, :] / both[k : k + 1, k : k + 1]
        both = jnp.where(row_ids == k, pivot_row, both - both[:, k : k + 1] * pivot_row)
    return lanes(both[:, size : 2 * size])


def kernel(
    sizes, q_hbm, spots_ref, spot_row_hbm, live_ref, cols_hbm, sims_hbm, sol_ref, res_ref,
    q_ref, spot_row_ref, cols_ref, sims_ref, blocks, colsum, rowsum, basis, vectors, scale,
    xc, xr, xc2, xr2, fwd, bwd, out_r, out_c, out_rb, out_cb,
    deg_r, deg_c, deg_rr, deg_cr, scl_r, scl_c,
    yr, relay_in, relay_out, zs, zr, rr, gram_e, gram_ei, gram_l, gram_li,
    in_s, ag_z, ag_sem, dg_sem, sc_sem, rs_relay, rs_y, rs_sem, ar_sem,
):
    R, Y, Z = sizes
    C = Y * Z
    RB, CB = R * PS, C * PS
    SLOTS = blocks.shape[0]
    shift = CB.bit_length() - 1
    a = lax.axis_index("row")
    b = lax.axis_index("col")
    y = b // Z
    z = b % Z

    def row_dev(k):
        return (lax.rem(a + k, R), b)

    def col_dev(k):
        return (a, lax.rem(b + k, C))

    def z_dev(k):
        return (a, y * Z + lax.rem(z + k, Z))

    def y_dev(k):
        return (a, lax.rem(y + k, Y) * Z + z)

    def copy(src, dst, ss, rs, dev):
        return pltpu.make_async_remote_copy(
            src_ref=src, dst_ref=dst, send_sem=ss, recv_sem=rs, device_id=dev, device_id_type=MESH
        )

    barrier = pltpu.get_barrier_semaphore()
    for k in range(1, R):
        pl.semaphore_signal(barrier, inc=1, device_id=row_dev(k), device_id_type=MESH)
    for k in range(1, C):
        pl.semaphore_signal(barrier, inc=1, device_id=col_dev(k), device_id_type=MESH)

    quarter = SLOTS // 4
    loads = []
    for n in range(4):
        part = pl.ds(n * quarter, quarter)
        loads.append(
            (
                pltpu.make_async_copy(cols_hbm.at[part], cols_ref.at[part], in_s.at[n]),
                pltpu.make_async_copy(sims_hbm.at[part], sims_ref.at[part], in_s.at[4 + n]),
            )
        )
    others = (
        pltpu.make_async_copy(q_hbm, q_ref, in_s.at[8]),
        pltpu.make_async_copy(spot_row_hbm, spot_row_ref, in_s.at[9]),
    )
    for c in [*others, *loads[0], *loads[1], *loads[2], *loads[3]]:
        c.start()

    near_first = sorted(range(1, Z), key=lambda k: (min(k, Z - k), k))

    class Gather:
        def __init__(self, turn, col_buf, row_buf):
            self.turn, self.col_buf, self.row_buf = turn, col_buf, row_buf
            mine_c = col_buf.at[pl.ds(b * PS, PS)]
            mine_r = row_buf.at[pl.ds(a * PS, PS)]
            col_sent, row_sent, y_got, row_got = [ag_sem.at[turn, n] for n in range(4)]
            self.row = [copy(mine_r, mine_r, row_sent, row_got, row_dev(k)) for k in range(1, R)]
            self.z = {k: copy(mine_c, mine_c, col_sent, ag_z.at[turn, k], z_dev(k)) for k in range(1, Z)}
            self.y = {}
            for kz in range(Z):
                chunk = col_buf.at[pl.ds((y * Z + lax.rem(z - kz + Z, Z)) * PS, PS)]
                self.y[kz] = [
                    copy(chunk, chunk, col_sent, y_got, y_dev(ky)) for ky in ((2, 1, 3) if Y == 4 else (1,))
                ]

        def start(self):
            for c in self.y[0]:
                c.start()
            for kz in near_first:
                self.z[kz].start()
            for c in self.row:
                c.start()

        def forward(self):
            for kz in near_first:
                self.z[kz].wait_recv()
                for c in self.y[kz]:
                    c.start()

        def finish_row(self):
            wait_all(self.row_buf.at[pl.ds(0, (R - 1) * PS)], ag_sem.at[self.turn, 3])
            wait_all(self.row_buf.at[pl.ds(0, (R - 1) * PS)], ag_sem.at[self.turn, 1])

        def finish_col(self):
            wait_all(self.col_buf.at[pl.ds(0, (Y - 1) * Z * PS)], ag_sem.at[self.turn, 2])
            wait_all(self.col_buf.at[pl.ds(0, (C - 1) * PS)], ag_sem.at[self.turn, 0])

    gather1 = Gather(0, xc, xr)

    lane_ids = lax.broadcasted_iota(jnp.int32, (128, 128), 0).astype(jnp.int16)
    halves = (
        lax.broadcasted_iota(jnp.int32, (8, 256), 0)
        == lax.shift_right_logical(lax.broadcasted_iota(jnp.int32, (8, 256), 1), 7)
    )
    halves = jnp.where(halves, 1.0, 0.0).astype(BF16)

    def build(s):
        idx = cols_ref[s]
        sim = sims_ref[s].astype(F32)
        value = jnp.zeros(sim.shape, F32)
        for t in range(idx.shape[0]):
            value = value + jnp.where(idx == idx[t : t + 1], sim[t : t + 1], 0.0)
        value = value.astype(BF16)
        idx = idx.astype(jnp.int16)
        block = jnp.zeros((128, 128), BF16)
        for t in range(idx.shape[0]):
            here = lane_ids == jnp.broadcast_to(idx[t : t + 1], (128, 128))
            block = jnp.where(here, jnp.broadcast_to(value[t : t + 1], (128, 128)), block)
        blocks[s] = block
        rowsum[pl.ds(s, 1), :] = jnp.sum(sim, axis=0, keepdims=True)
        return block

    def build_turn(g, carry):
        turns = SLOTS // BUILD
        for n in range(4):

            @pl.when(g == n * turns // 4)
            def _():
                for c in loads[n]:
                    c.wait()

        @pl.when(g == turns // 2)
        def _():
            gather1.forward()

        for u in range(0, BUILD, 4):
            s = g * BUILD + u
            four = [build(s + v) for v in range(4)]
            pairs = jnp.concatenate(
                [jnp.concatenate([four[0], four[2]], 1), jnp.concatenate([four[1], four[3]], 1)], 0
            )
            sums = mm(halves, pairs, True)
            colsum[pl.ds(s, 1), :] = sums[0:1, 0:128]
            colsum[pl.ds(s + 1, 1), :] = sums[0:1, 128:256]
            colsum[pl.ds(s + 2, 1), :] = sums[1:2, 0:128]
            colsum[pl.ds(s + 3, 1), :] = sums[1:2, 128:256]
        return carry

    for c in others:
        c.wait()
    basis[32:128, :] = jnp.zeros((96, PS * 128), F32)
    for p in range(PS):
        part = q_ref[:, p * 128 : (p + 1) * 128]
        basis[0:32, p * 128 : (p + 1) * 128] = part
        xc[b * PS + p] = part.astype(BF16)
        xr[a * PS + p] = part.astype(BF16)
    pl.semaphore_wait(barrier, R - 1 + C - 1)
    gather1.start()
    lax.fori_loop(0, SLOTS // BUILD, build_turn, 0)

    spot_row = spot_row_ref[...]
    live = live_ref[0, 0]
    used = lax.broadcasted_iota(jnp.int32, (1, SLOTS), 1) < live
    in_row = (lax.shift_right_logical(spot_row, shift) == lax.broadcasted_iota(jnp.int32, (RB, SLOTS), 0)) & used
    in_col = ((spot_row & (CB - 1)) == lax.broadcasted_iota(jnp.int32, (CB, SLOTS), 0)) & used
    in_row_f = jnp.where(in_row, 1.0, 0.0).astype(F32)
    in_col_f = jnp.where(in_col, 1.0, 0.0).astype(F32)
    row_degree = mm_high(in_row_f, rowsum[...])
    col_degree = mm_high(in_col_f, colsum[...])
    for g in range(R):
        deg_r[g] = row_degree[g * PS : (g + 1) * PS]
    for g in range(C):
        deg_c[g] = col_degree[g * PS : (g + 1) * PS]
    for k in range(1, C):
        copy(deg_c.at[lax.rem(b + k, C)], deg_cr.at[k], dg_sem.at[0], dg_sem.at[1], col_dev(k)).start()
    for k in range(1, R):
        copy(deg_r.at[lax.rem(a + k, R)], deg_rr.at[k], dg_sem.at[2], dg_sem.at[3], row_dev(k)).start()
    degree = deg_r[a] + deg_c[b]
    wait_all(deg_rr.at[pl.ds(1, R - 1)], dg_sem.at[3])
    wait_all(deg_cr.at[pl.ds(1, C - 1)], dg_sem.at[1])
    for k in range(1, C):
        degree = degree + deg_cr[k]
    for k in range(1, R):
        degree = degree + deg_rr[k]
    degree = 1.0 + 0.5 * degree
    scaling = 1.0 / jnp.sqrt(degree)
    scl_r[a] = scaling
    scl_c[b] = scaling
    scale[...] = scaling
    for k in range(1, C):
        copy(scl_c.at[b], scl_c.at[b], sc_sem.at[0], sc_sem.at[1], col_dev(k)).start()
    for k in range(1, R):
        copy(scl_r.at[a], scl_r.at[a], sc_sem.at[2], sc_sem.at[3], row_dev(k)).start()
    gather1.finish_row()
    wait_all(deg_rr.at[pl.ds(1, R - 1)], dg_sem.at[2])
    wait_all(deg_cr.at[pl.ds(1, C - 1)], dg_sem.at[0])
    for n in range(2):
        wait_all(scl_r.at[pl.ds(0, R - 1)], sc_sem.at[2 + n])

    def scale_part(buf, scl, g):
        factors = scl[g]
        for p in range(PS):
            buf[g * PS + p] = (buf[g * PS + p].astype(F32) * factors[p : p + 1]).astype(BF16)

    def scale_cols(g, carry):
        scale_part(xc, scl_c, g)
        return carry

    def scale_rows(g, carry):
        scale_part(xr, scl_r, g)
        return carry

    lax.fori_loop(0, R, scale_rows, 0)

    def spread(x):
        zero = jnp.zeros((32, 128), BF16)
        pairs = [(x[0], zero), (x[1], zero), (zero, x[2]), (zero, x[3])]
        return jnp.concatenate([jnp.concatenate(pair, 1) for pair in pairs], 0)

    def square(x):
        return jnp.concatenate([jnp.concatenate(x[0:2], 1), jnp.concatenate(x[2:4], 1)], 0)

    def back_four(s, row_buf):
        x = [row_buf[lax.shift_right_logical(spots_ref[s + n], shift)] for n in range(4)]
        out = mm(spread(x), square([blocks[s], blocks[s + 2], blocks[s + 1], blocks[s + 3]]), True)
        for n in range(4):
            bwd[:, s + n, :] = out[32 * n : 32 * n + 32, 128 * (n & 1) : 128 * (n & 1) + 128]

    def ahead_four(s, col_buf):
        x = [col_buf[spots_ref[s + n] & (CB - 1)] for n in range(4)]
        out = mm(spread(x), square([blocks[s + n] for n in range(4)]))
        for n in range(4):
            fwd[:, s + n, :] = out[32 * n : 32 * n + 32, 128 * (n & 1) : 128 * (n & 1) + 128]

    def products(four, buf, low, high):
        def turn(g, carry):
            for u in range(UNROLL):
                four((g * UNROLL + u) * 4, buf)
            return carry

        lax.fori_loop(low // (4 * UNROLL), high // (4 * UNROLL), turn, 0)

    pick_r = in_row_f.astype(BF16)
    pick_c = in_col_f.astype(BF16)

    def gather_sum(pick, terms):
        high = terms.astype(BF16)
        low = (terms - high.astype(F32)).astype(BF16)
        return mm(pick, high) + mm(pick, low)

    def col_part():
        for m in range(32):
            out_c[:, m, :] = gather_sum(pick_c, bwd[m])

        def to_wire(v, carry):
            for p in range(2 * PS):
                out_cb[v * 2 * PS + p] = out_c[v * 2 * PS + p].astype(BF16)
            return carry

        lax.fori_loop(0, C // 2, to_wire, 0)

    def row_part():
        for m in range(32):
            out_r[:, m, :] = gather_sum(pick_r, fwd[m])
        for v in range(RB):
            out_rb[v] = out_r[v].astype(BF16)

    ways = (1, Y - 1) if Y == 4 else (1,)

    def relay_way(kz):
        return 0 if kz % 2 == 0 else 1

    places = [lax.rem(z + kz, Z) for kz in range(Z)]
    order = list(reversed(near_first)) + [0]

    def target(ky, kz):
        return pl.ds((lax.rem(y + ky, Y) * Z + places[kz]) * PS, PS)

    def half(turn, src, kz, w):
        copy(src, yr.at[turn, kz, w], rs_sem.at[turn, 0], rs_y.at[turn, kz], y_dev(ways[w])).start()

    def start_col_sum(turn):
        relays = {}
        if Y == 4:
            for kz in order:
                relays[kz] = copy(
                    out_cb.at[target(2, kz)],
                    relay_in.at[turn, kz],
                    rs_sem.at[turn, 0],
                    rs_relay.at[turn, kz],
                    y_dev(ways[relay_way(kz)]),
                )
                relays[kz].start()
        for kz in order:
            for w, ky in enumerate(ways):
                if Y != 4 or w != relay_way(kz):
                    half(turn, out_cb.at[target(ky, kz)], kz, w)
        return relays

    def start_row_sum(turn):
        for k in range(1, R):
            src = out_rb.at[pl.ds(lax.rem(a + k, R) * PS, PS)]
            copy(src, rr.at[turn, k], rs_sem.at[turn, 3], rs_sem.at[turn, 4], row_dev(k)).start()

    def finish_sums(turn, relays, beside=(None, None)):
        y_sent, z_sent, z_got, row_sent, row_got = [rs_sem.at[turn, n] for n in range(5)]
        if Y == 4:
            for kz in order:
                w = relay_way(kz)
                relays[kz].wait_recv()
                total = out_c[target(ways[w], kz)] + relay_in[turn, kz].astype(F32)
                relay_out[turn, kz] = total.astype(BF16)
                half(turn, relay_out.at[turn, kz], kz, w)
        if beside[0]:
            beside[0]()
        own = out_r[pl.ds(a * PS, PS)]
        for kz in order:
            total = out_c[target(0, kz)]
            wait_all(yr.at[turn, kz], rs_y.at[turn, kz])
            for w in range(len(ways)):
                total = total + yr[turn, kz, w].astype(F32)
            if kz:
                zs[turn, kz] = total.astype(BF16)
                copy(zs.at[turn, kz], zr.at[turn, kz], z_sent, z_got, z_dev(kz)).start()
            else:
                own = own + total
        result = beside[1]() if beside[1] else None
        wait_all(rr.at[turn, pl.ds(1, R - 1)], row_got)
        for k in range(1, R):
            own = own + rr[turn, k].astype(F32)
        wait_all(zr.at[turn, pl.ds(1, Z - 1)], z_got)
        for kz in range(1, Z):
            own = own + zr[turn, kz].astype(F32)
        wait_all(out_cb.at[pl.ds(0, (Y - 1) * Z * PS)], y_sent)
        wait_all(rr.at[turn, pl.ds(1, R - 1)], row_sent)
        wait_all(zr.at[turn, pl.ds(1, Z - 1)], z_sent)
        return own, result

    class Reduce:
        def __init__(self, turn, buf, buf_in):
            self.turn, self.buf, self.buf_in = turn, buf, buf_in

        def start(self, stage, value):
            count, dev = ((R, row_dev), (Z, z_dev), (Y, y_dev))[stage]
            self.buf[stage] = value
            for k in range(1, count):
                copy(
                    self.buf.at[stage],
                    self.buf_in.at[stage, k],
                    ar_sem.at[self.turn, stage, 0],
                    ar_sem.at[self.turn, stage, 1],
                    dev(k),
                ).start()

        def finish(self, stage):
            count = (R, Z, Y)[stage]
            there = self.buf_in.at[stage, pl.ds(1, count - 1)]
            wait_all(there, ar_sem.at[self.turn, stage, 1])
            total = self.buf[stage]
            for k in range(1, count):
                total = total + self.buf_in[stage, k]
            wait_all(there, ar_sem.at[self.turn, stage, 0])
            return total

    products(back_four, xr, 0, SLOTS)
    col_part()
    relays = start_col_sum(0)
    for n in range(2):
        wait_all(scl_c.at[pl.ds(0, C - 1)], sc_sem.at[n])
    gather1.finish_col()
    lax.fori_loop(0, C, scale_cols, 0)
    products(ahead_four, xc, 0, SLOTS)
    row_part()
    start_row_sum(0)
    summed, _ = finish_sums(0, relays)
    scaling = scale[...]
    for p in range(PS):
        u1 = (0.5 * WEIGHT) * scaling[p : p + 1] * summed[p]
        basis[32:64, p * 128 : (p + 1) * 128] = u1
        part = (scaling[p : p + 1] * u1).astype(BF16)
        xc2[b * PS + p] = part
        xr2[a * PS + p] = part
    gather2 = Gather(1, xc2, xr2)
    gather2.start()
    early = Reduce(0, gram_e, gram_ei)
    g0 = mm_high(basis[0:64, :], basis[0:64, :], True)
    early.start(
        0, jnp.concatenate([pack(g0[0:32]), pack(g0[0:32, 32:64]), pack(g0[32:64, 32:64])], axis=0)
    )
    gather2.finish_row()
    products(back_four, xr2, 0, SLOTS // 2)
    gather2.forward()
    early.start(1, early.finish(0))
    products(back_four, xr2, SLOTS // 2, SLOTS)
    col_part()
    relays = start_col_sum(1)
    early.start(2, early.finish(1))
    gather2.finish_col()
    products(ahead_four, xc2, 0, SLOTS)
    row_part()
    start_row_sum(1)

    held = {}

    def first_inverses():
        grams = early.finish(2)
        g00 = symmetric(unpack(grams[0:8]))
        g01 = unpack(grams[8:16])
        g11 = symmetric(unpack(grams[16:24]))
        s01 = symmetric(g01)
        inv_curve = inverse(g00 - s01)
        inv_gram = inverse(g00)
        held["all"] = g00, g01, g11, s01, inv_curve, inv_gram

    def first_systems():
        g00, g01, g11, s01, inv_curve, inv_gram = held["all"]
        p1 = small_mm(g00, inv_curve)
        p0 = -small_mm(s01, inv_curve)
        p0_t, p1_t = flip(p0), flip(p1)
        newgram = small_mm(small_mm(p0, g00), p0_t) + small_mm(small_mm(p1, g11), p1_t)
        newgram = symmetric(newgram + 2.0 * small_mm(small_mm(p0, g01), p1_t))
        d0 = p0 + small_mm(newgram, inv_gram)
        direction = lanes(d0[:, 0:32], p1[:, 0:32])
        applied = lanes(d0[:, 0:32], p1[:, 0:32] - d0[:, 0:32], -p1[:, 0:32])
        whole = jnp.concatenate(
            [
                lanes(g00[:, 0:32], g01[:, 0:32], g11[:, 0:32]),
                lanes(flip(g01)[:, 0:32], g11[:, 0:32]),
            ],
            axis=0,
        )
        known = small_mm(direction, mm_high(whole, tall(applied).T))
        coef = jnp.concatenate([direction, lanes(p0[:, 0:32], p1[:, 0:32]), p1], axis=0)
        vectors[...] = mm_high(coef, basis[...])
        return newgram, p1, p1_t, applied, known

    summed, small = finish_sums(1, relays, (first_inverses, first_systems))
    newgram, p1, p1_t, applied, known = small
    scaling = scale[...]
    for p in range(PS):
        u2 = (0.5 * WEIGHT) * scaling[p : p + 1] * summed[p]
        basis[64:96, p * 128 : (p + 1) * 128] = u2
    late = Reduce(1, gram_l, gram_li)
    late.start(0, pack(mm_high(basis[32:64, :], basis[64:96, :], True)))
    image = mm_high(applied, basis[...])
    late.start(1, late.finish(0))
    late.start(2, late.finish(1))
    g12 = unpack(late.finish(2))
    curve = symmetric(known - small_mm(small_mm(p1, g12), p1_t))
    steps = small_mm(newgram, inverse(curve))
    sol_ref[...] = vectors[64:96, :] + mm_high(steps, tall(vectors[0:32, :]))
    res_ref[...] = vectors[32:64, :] - mm_high(steps, tall(image))


def split_col(count):
    return (4, count // 4) if count >= 8 else (2, count // 2)


def solution(mesh):
    R, C = mesh.shape["row"], mesh.shape["col"]
    Y, Z = split_col(C)
    RB, CB = R * PS, C * PS

    def body(queries, block_spots, live_blocks, neighbor_cols, neighbor_sims):
        slots = block_spots.shape[2]
        vmem = pltpu.VMEM
        sems = pltpu.SemaphoreType.DMA
        ways = 2 if Y == 4 else 1
        scratch = [
            vmem(queries.shape, F32), vmem((1, slots), jnp.int32),
            vmem(neighbor_cols.shape[2:], jnp.int32), vmem(neighbor_sims.shape[2:], BF16),
            vmem((slots, 128, 128), BF16), vmem((slots, 128), F32), vmem((slots, 128), F32),
            vmem((128, PS * 128), F32), vmem((96, PS * 128), F32), vmem((PS, 128), F32),
            vmem((CB, 32, 128), BF16), vmem((RB, 32, 128), BF16),
            vmem((CB, 32, 128), BF16), vmem((RB, 32, 128), BF16),
            vmem((32, slots, 128), F32), vmem((32, slots, 128), F32),
            vmem((RB, 32, 128), F32), vmem((CB, 32, 128), F32),
            vmem((RB, 32, 128), BF16), vmem((CB, 32, 128), BF16),
            vmem((R, PS, 128), F32), vmem((C, PS, 128), F32),
            vmem((R, PS, 128), F32), vmem((C, PS, 128), F32),
            vmem((R, PS, 128), F32), vmem((C, PS, 128), F32),
            vmem((2, Z, ways, PS, 32, 128), BF16), vmem((2, Z, PS, 32, 128), BF16),
            vmem((2, Z, PS, 32, 128), BF16), vmem((2, Z, PS, 32, 128), BF16),
            vmem((2, Z, PS, 32, 128), BF16), vmem((2, R, PS, 32, 128), BF16),
            vmem((3, 24, 128), F32), vmem((3, max(R, Z, Y), 24, 128), F32),
            vmem((3, 8, 128), F32), vmem((3, max(R, Z, Y), 8, 128), F32),
            sems((10,)), sems((2, Z)), sems((2, 4)), sems((4,)), sems((4,)),
            sems((2, Z)), sems((2, Z)), sems((2, 5)), sems((2, 3, 2)),
        ]
        in_vmem = pl.BlockSpec(memory_space=pltpu.VMEM)
        in_any = pl.BlockSpec(memory_space=pl.ANY)
        in_smem = pl.BlockSpec(memory_space=pltpu.SMEM)
        shape = jax.ShapeDtypeStruct(queries.shape, F32)
        return pl.pallas_call(
            functools.partial(kernel, (R, Y, Z)),
            out_shape=(shape, shape),
            in_specs=[in_any, in_smem, in_any, in_smem, in_any, in_any],
            out_specs=(in_vmem, in_vmem),
            scratch_shapes=scratch,
            compiler_params=pltpu.CompilerParams(
                collective_id=0, has_side_effects=True, vmem_limit_bytes=53 * 1024 * 1024 + 512 * 1024
            ),
        )(
            queries,
            block_spots[0, 0],
            block_spots[0],
            live_blocks,
            neighbor_cols[0, 0],
            neighbor_sims[0, 0],
        )

    placed = (
        P(None, ("row", "col")),
        P("row", "col", None),
        P("row", "col"),
        P("row", "col", None, None, None),
        P("row", "col", None, None, None),
    )
    return jax.shard_map(
        body,
        mesh=mesh,
        in_specs=placed,
        out_specs=(P(None, ("row", "col")), P(None, ("row", "col"))),
        check_vma=False,
    )
```

```python
import functools

import jax
import jax.numpy as jnp
from jax import lax
from jax.experimental import pallas as pl
from jax.experimental.pallas import tpu as pltpu
from jax.sharding import PartitionSpec as P

MESH = pl.DeviceIdType.MESH
HIGH = lax.Precision.HIGHEST
F32 = jnp.float32
BF16 = jnp.bfloat16
WEIGHT = 0.95
PS = 4
UNROLL = 4
BUILD = 16


def mm(first, second, transposed=False):
    dims = (((1,), (1 if transposed else 0,)), ((), ()))
    return lax.dot_general(first, second, dims, preferred_element_type=F32)


def mm_high(first, second, transposed=False):
    dims = (((1,), (1 if transposed else 0,)), ((), ()))
    return lax.dot_general(first, second, dims, precision=HIGH, preferred_element_type=F32)


def lanes(*parts):
    width = sum(p.shape[1] for p in parts)
    return jnp.concatenate(list(parts) + [jnp.zeros((parts[0].shape[0], 128 - width), F32)], axis=1)


def tall(small):
    return jnp.concatenate([small, jnp.zeros((128 - small.shape[0], small.shape[1]), F32)], axis=0)


def pack(square):
    return jnp.concatenate([square[8 * i : 8 * i + 8, 0:32] for i in range(4)], axis=1)


def unpack(packed):
    return lanes(jnp.concatenate([packed[:, 32 * i : 32 * i + 32] for i in range(4)], axis=0))


def wait_all(ref, sem):
    pltpu.make_async_copy(ref, ref, sem).wait()


def flip(small):
    return tall(small).T[0:32]


def symmetric(small):
    return 0.5 * (small + flip(small))


def small_mm(first, second):
    return mm_high(first, tall(second))


def inverse(small):
    size = small.shape[0]
    row_ids = lax.broadcasted_iota(jnp.int32, small.shape, 0)
    lane_ids = lax.broadcasted_iota(jnp.int32, small.shape, 1)
    both = small + (row_ids + size == lane_ids).astype(F32)
    for k in range(size):
        pivot_row = both[k : k + 1, :] / both[k : k + 1, k : k + 1]
        both = jnp.where(row_ids == k, pivot_row, both - both[:, k : k + 1] * pivot_row)
    return lanes(both[:, size : 2 * size])


def kernel(
    sizes, q_hbm, spots_ref, spot_row_hbm, live_ref, cols_hbm, sims_hbm, sol_ref, res_ref,
    q_ref, spot_row_ref, cols_ref, sims_ref, blocks, colsum, rowsum, basis, vectors, scale,
    xc, xr, xc2, xr2, fwd, bwd, out_r, out_c, out_rb, out_cb,
    deg_r, deg_c, deg_rr, deg_cr, scl_r, scl_c,
    yr, relay_in, relay_out, zs, zr, rr, gram_e, gram_ei, gram_l, gram_li,
    in_s, ag_z, ag_sem, dg_sem, sc_sem, rs_relay, rs_y, rs_sem, ar_sem,
):
    R, Y, Z = sizes
    C = Y * Z
    RB, CB = R * PS, C * PS
    SLOTS = blocks.shape[0]
    shift = CB.bit_length() - 1
    a = lax.axis_index("row")
    b = lax.axis_index("col")
    y = b // Z
    z = b % Z

    def row_dev(k):
        return (lax.rem(a + k, R), b)

    def col_dev(k):
        return (a, lax.rem(b + k, C))

    def z_dev(k):
        return (a, y * Z + lax.rem(z + k, Z))

    def y_dev(k):
        return (a, lax.rem(y + k, Y) * Z + z)

    def copy(src, dst, ss, rs, dev):
        return pltpu.make_async_remote_copy(
            src_ref=src, dst_ref=dst, send_sem=ss, recv_sem=rs, device_id=dev, device_id_type=MESH
        )

    barrier = pltpu.get_barrier_semaphore()
    for k in range(1, R):
        pl.semaphore_signal(barrier, inc=1, device_id=row_dev(k), device_id_type=MESH)
    for k in range(1, C):
        pl.semaphore_signal(barrier, inc=1, device_id=col_dev(k), device_id_type=MESH)

    quarter = SLOTS // 4
    loads = []
    for n in range(4):
        part = pl.ds(n * quarter, quarter)
        loads.append(
            (
                pltpu.make_async_copy(cols_hbm.at[part], cols_ref.at[part], in_s.at[n]),
                pltpu.make_async_copy(sims_hbm.at[part], sims_ref.at[part], in_s.at[4 + n]),
            )
        )
    others = (
        pltpu.make_async_copy(q_hbm, q_ref, in_s.at[8]),
        pltpu.make_async_copy(spot_row_hbm, spot_row_ref, in_s.at[9]),
    )
    for c in [*others, *loads[0], *loads[1], *loads[2], *loads[3]]:
        c.start()

    near_first = sorted(range(1, Z), key=lambda k: (min(k, Z - k), k))

    class Gather:
        def __init__(self, turn, col_buf, row_buf):
            self.turn, self.col_buf, self.row_buf = turn, col_buf, row_buf
            mine_c = col_buf.at[pl.ds(b * PS, PS)]
            mine_r = row_buf.at[pl.ds(a * PS, PS)]
            col_sent, row_sent, y_got, row_got = [ag_sem.at[turn, n] for n in range(4)]
            self.row = [copy(mine_r, mine_r, row_sent, row_got, row_dev(k)) for k in range(1, R)]
            self.z = {k: copy(mine_c, mine_c, col_sent, ag_z.at[turn, k], z_dev(k)) for k in range(1, Z)}
            self.y = {}
            for kz in range(Z):
                chunk = col_buf.at[pl.ds((y * Z + lax.rem(z - kz + Z, Z)) * PS, PS)]
                self.y[kz] = [
                    copy(chunk, chunk, col_sent, y_got, y_dev(ky)) for ky in ((2, 1, 3) if Y == 4 else (1,))
                ]

        def start(self):
            for c in self.y[0]:
                c.start()
            for kz in near_first:
                self.z[kz].start()
            for c in self.row:
                c.start()

        def forward(self, first=0, last=None):
            for kz in near_first[first:last]:
                self.z[kz].wait_recv()
                for c in self.y[kz]:
                    c.start()

        def finish_row(self):
            wait_all(self.row_buf.at[pl.ds(0, (R - 1) * PS)], ag_sem.at[self.turn, 3])
            wait_all(self.row_buf.at[pl.ds(0, (R - 1) * PS)], ag_sem.at[self.turn, 1])

        def finish_col(self):
            wait_all(self.col_buf.at[pl.ds(0, (Y - 1) * Z * PS)], ag_sem.at[self.turn, 2])
            wait_all(self.col_buf.at[pl.ds(0, (C - 1) * PS)], ag_sem.at[self.turn, 0])

    gather1 = Gather(0, xc, xr)

    lane_ids = lax.broadcasted_iota(jnp.int32, (128, 128), 0).astype(jnp.int16)
    halves = (
        lax.broadcasted_iota(jnp.int32, (8, 256), 0)
        == lax.shift_right_logical(lax.broadcasted_iota(jnp.int32, (8, 256), 1), 7)
    )
    halves = jnp.where(halves, 1.0, 0.0).astype(BF16)

    def build(s):
        idx = cols_ref[s]
        sim = sims_ref[s].astype(F32)
        value = jnp.zeros(sim.shape, F32)
        for t in range(idx.shape[0]):
            value = value + jnp.where(idx == idx[t : t + 1], sim[t : t + 1], 0.0)
        value = value.astype(BF16)
        idx = idx.astype(jnp.int16)
        block = jnp.zeros((128, 128), BF16)
        for t in range(idx.shape[0]):
            here = lane_ids == jnp.broadcast_to(idx[t : t + 1], (128, 128))
            block = jnp.where(here, jnp.broadcast_to(value[t : t + 1], (128, 128)), block)
        blocks[s] = block
        rowsum[pl.ds(s, 1), :] = jnp.sum(sim, axis=0, keepdims=True)
        return block

    def build_turn(g, carry):
        turns = SLOTS // BUILD
        for n in range(4):

            @pl.when(g == n * turns // 4)
            def _():
                for c in loads[n]:
                    c.wait()

        @pl.when(g == turns // 2)
        def _():
            gather1.forward()

        for u in range(0, BUILD, 4):
            s = g * BUILD + u
            four = [build(s + v) for v in range(4)]
            pairs = jnp.concatenate(
                [jnp.concatenate([four[0], four[2]], 1), jnp.concatenate([four[1], four[3]], 1)], 0
            )
            sums = mm(halves, pairs, True)
            colsum[pl.ds(s, 1), :] = sums[0:1, 0:128]
            colsum[pl.ds(s + 1, 1), :] = sums[0:1, 128:256]
            colsum[pl.ds(s + 2, 1), :] = sums[1:2, 0:128]
            colsum[pl.ds(s + 3, 1), :] = sums[1:2, 128:256]
        return carry

    for c in others:
        c.wait()
    basis[32:128, :] = jnp.zeros((96, PS * 128), F32)
    for p in range(PS):
        part = q_ref[:, p * 128 : (p + 1) * 128]
        basis[0:32, p * 128 : (p + 1) * 128] = part
        xc[b * PS + p] = part.astype(BF16)
        xr[a * PS + p] = part.astype(BF16)
    pl.semaphore_wait(barrier, R - 1 + C - 1)
    gather1.start()
    lax.fori_loop(0, SLOTS // BUILD, build_turn, 0)

    spot_row = spot_row_ref[...]
    live = live_ref[0, 0]
    used = lax.broadcasted_iota(jnp.int32, (1, SLOTS), 1) < live
    in_row = (lax.shift_right_logical(spot_row, shift) == lax.broadcasted_iota(jnp.int32, (RB, SLOTS), 0)) & used
    in_col = ((spot_row & (CB - 1)) == lax.broadcasted_iota(jnp.int32, (CB, SLOTS), 0)) & used
    in_row_f = jnp.where(in_row, 1.0, 0.0).astype(F32)
    in_col_f = jnp.where(in_col, 1.0, 0.0).astype(F32)
    row_degree = mm_high(in_row_f, rowsum[...])
    col_degree = mm_high(in_col_f, colsum[...])
    for g in range(R):
        deg_r[g] = row_degree[g * PS : (g + 1) * PS]
    for g in range(C):
        deg_c[g] = col_degree[g * PS : (g + 1) * PS]
    for k in range(1, C):
        copy(deg_c.at[lax.rem(b + k, C)], deg_cr.at[k], dg_sem.at[0], dg_sem.at[1], col_dev(k)).start()
    for k in range(1, R):
        copy(deg_r.at[lax.rem(a + k, R)], deg_rr.at[k], dg_sem.at[2], dg_sem.at[3], row_dev(k)).start()
    degree = deg_r[a] + deg_c[b]
    wait_all(deg_rr.at[pl.ds(1, R - 1)], dg_sem.at[3])
    wait_all(deg_cr.at[pl.ds(1, C - 1)], dg_sem.at[1])
    for k in range(1, C):
        degree = degree + deg_cr[k]
    for k in range(1, R):
        degree = degree + deg_rr[k]
    degree = 1.0 + 0.5 * degree
    scaling = 1.0 / jnp.sqrt(degree)
    scl_r[a] = scaling
    scl_c[b] = scaling
    scale[...] = scaling
    for k in range(1, R):
        copy(scl_r.at[a], scl_r.at[a], sc_sem.at[2], sc_sem.at[3], row_dev(k)).start()
    for k in range(1, C):
        copy(scl_c.at[b], scl_c.at[b], sc_sem.at[0], sc_sem.at[1], col_dev(k)).start()
    gather1.finish_row()
    wait_all(deg_rr.at[pl.ds(1, R - 1)], dg_sem.at[2])
    wait_all(deg_cr.at[pl.ds(1, C - 1)], dg_sem.at[0])
    for n in range(2):
        wait_all(scl_r.at[pl.ds(0, R - 1)], sc_sem.at[2 + n])

    def scale_part(buf, scl, g):
        factors = scl[g]
        for p in range(PS):
            buf[g * PS + p] = (buf[g * PS + p].astype(F32) * factors[p : p + 1]).astype(BF16)

    def scale_cols(g, carry):
        scale_part(xc, scl_c, g)
        return carry

    def scale_rows(g, carry):
        scale_part(xr, scl_r, g)
        return carry

    lax.fori_loop(0, R, scale_rows, 0)

    def spread(x):
        zero = jnp.zeros((32, 128), BF16)
        pairs = [(x[0], zero), (x[1], zero), (zero, x[2]), (zero, x[3])]
        return jnp.concatenate([jnp.concatenate(pair, 1) for pair in pairs], 0)

    def square(x):
        return jnp.concatenate([jnp.concatenate(x[0:2], 1), jnp.concatenate(x[2:4], 1)], 0)

    def back_four(s, row_buf):
        x = [row_buf[lax.shift_right_logical(spots_ref[s + n], shift)] for n in range(4)]
        out = mm(spread(x), square([blocks[s], blocks[s + 2], blocks[s + 1], blocks[s + 3]]), True)
        for n in range(4):
            bwd[:, s + n, :] = out[32 * n : 32 * n + 32, 128 * (n & 1) : 128 * (n & 1) + 128]

    def ahead_four(s, col_buf):
        x = [col_buf[spots_ref[s + n] & (CB - 1)] for n in range(4)]
        out = mm(spread(x), square([blocks[s + n] for n in range(4)]))
        for n in range(4):
            fwd[:, s + n, :] = out[32 * n : 32 * n + 32, 128 * (n & 1) : 128 * (n & 1) + 128]

    def products(four, buf, low, high):
        def turn(g, carry):
            for u in range(UNROLL):
                four((g * UNROLL + u) * 4, buf)
            return carry

        lax.fori_loop(low // (4 * UNROLL), high // (4 * UNROLL), turn, 0)

    pick_r = in_row_f.astype(BF16)
    pick_c = in_col_f.astype(BF16)

    def gather_sum(pick, terms):
        high = terms.astype(BF16)
        low = (terms - high.astype(F32)).astype(BF16)
        return mm(pick, high) + mm(pick, low)

    def col_part():
        for m in range(32):
            out_c[:, m, :] = gather_sum(pick_c, bwd[m])

        def to_wire(v, carry):
            for p in range(2 * PS):
                out_cb[v * 2 * PS + p] = out_c[v * 2 * PS + p].astype(BF16)
            return carry

        lax.fori_loop(0, C // 2, to_wire, 0)

    def row_part():
        for m in range(32):
            out_r[:, m, :] = gather_sum(pick_r, fwd[m])
        for v in range(RB):
            out_rb[v] = out_r[v].astype(BF16)

    ways = (1, Y - 1) if Y == 4 else (1,)

    def relay_way(kz):
        return 0 if kz % 2 == 0 else 1

    places = [lax.rem(z + kz, Z) for kz in range(Z)]
    order = list(reversed(near_first)) + [0]

    def target(ky, kz):
        return pl.ds((lax.rem(y + ky, Y) * Z + places[kz]) * PS, PS)

    def half(turn, src, kz, w):
        copy(src, yr.at[turn, kz, w], rs_sem.at[turn, 0], rs_y.at[turn, kz], y_dev(ways[w])).start()

    def start_col_sum(turn):
        relays = {}
        if Y == 4:
            for kz in order:
                relays[kz] = copy(
                    out_cb.at[target(2, kz)],
                    relay_in.at[turn, kz],
                    rs_sem.at[turn, 0],
                    rs_relay.at[turn, kz],
                    y_dev(ways[relay_way(kz)]),
                )
                relays[kz].start()
        for kz in order:
            for w, ky in enumerate(ways):
                if Y != 4 or w != relay_way(kz):
                    half(turn, out_cb.at[target(ky, kz)], kz, w)
        return relays

    def start_row_sum(turn):
        for k in range(1, R):
            src = out_rb.at[pl.ds(lax.rem(a + k, R) * PS, PS)]
            copy(src, rr.at[turn, k], rs_sem.at[turn, 3], rs_sem.at[turn, 4], row_dev(k)).start()

    def hand_on(turn, relays):
        for kz in relays:
            w = relay_way(kz)
            relays[kz].wait_recv()
            total = out_c[target(ways[w], kz)] + relay_in[turn, kz].astype(F32)
            relay_out[turn, kz] = total.astype(BF16)
            half(turn, relay_out.at[turn, kz], kz, w)

    def start_z_sum(turn):
        for kz in order:
            total = out_c[target(0, kz)]
            wait_all(yr.at[turn, kz], rs_y.at[turn, kz])
            for w in range(len(ways)):
                total = total + yr[turn, kz, w].astype(F32)
            if kz:
                zs[turn, kz] = total.astype(BF16)
                copy(
                    zs.at[turn, kz], zr.at[turn, kz], rs_sem.at[turn, 1], rs_sem.at[turn, 2], z_dev(kz)
                ).start()
        return total

    def finish_sums(turn, own):
        y_sent, z_sent, z_got, row_sent, row_got = [rs_sem.at[turn, n] for n in range(5)]
        own = own + out_r[pl.ds(a * PS, PS)]
        wait_all(zr.at[turn, pl.ds(1, Z - 1)], z_got)
        for kz in range(1, Z):
            own = own + zr[turn, kz].astype(F32)
        wait_all(rr.at[turn, pl.ds(1, R - 1)], row_got)
        for k in range(1, R):
            own = own + rr[turn, k].astype(F32)
        wait_all(out_cb.at[pl.ds(0, (Y - 1) * Z * PS)], y_sent)
        wait_all(rr.at[turn, pl.ds(1, R - 1)], row_sent)
        wait_all(zr.at[turn, pl.ds(1, Z - 1)], z_sent)
        return own

    class Reduce:
        def __init__(self, turn, buf, buf_in):
            self.turn, self.buf, self.buf_in = turn, buf, buf_in

        def start(self, stage, value):
            count, dev = ((R, row_dev), (Z, z_dev), (Y, y_dev))[stage]
            self.buf[stage] = value
            for k in range(1, count):
                copy(
                    self.buf.at[stage],
                    self.buf_in.at[stage, k],
                    ar_sem.at[self.turn, stage, 0],
                    ar_sem.at[self.turn, stage, 1],
                    dev(k),
                ).start()

        def finish(self, stage):
            count = (R, Z, Y)[stage]
            there = self.buf_in.at[stage, pl.ds(1, count - 1)]
            wait_all(there, ar_sem.at[self.turn, stage, 1])
            total = self.buf[stage]
            for k in range(1, count):
                total = total + self.buf_in[stage, k]
            wait_all(there, ar_sem.at[self.turn, stage, 0])
            return total

    products(back_four, xr, 0, SLOTS)
    col_part()
    relays = start_col_sum(0)
    for n in range(2):
        wait_all(scl_c.at[pl.ds(0, C - 1)], sc_sem.at[n])
    gather1.finish_col()
    lax.fori_loop(0, C, scale_cols, 0)
    products(ahead_four, xc, 0, SLOTS // 2)
    hand_on(0, relays)
    products(ahead_four, xc, SLOTS // 2, SLOTS)
    row_part()
    start_row_sum(0)
    summed = finish_sums(0, start_z_sum(0))
    scaling = scale[...]
    for p in range(PS):
        u1 = (0.5 * WEIGHT) * scaling[p : p + 1] * summed[p]
        basis[32:64, p * 128 : (p + 1) * 128] = u1
        part = (scaling[p : p + 1] * u1).astype(BF16)
        xc2[b * PS + p] = part
        xr2[a * PS + p] = part
    gather2 = Gather(1, xc2, xr2)
    gather2.start()
    early = Reduce(0, gram_e, gram_ei)
    g0 = mm_high(basis[0:64, :], basis[0:64, :], True)
    early.start(
        0, jnp.concatenate([pack(g0[0:32]), pack(g0[0:32, 32:64]), pack(g0[32:64, 32:64])], axis=0)
    )
    gather2.forward(0, 2)
    gather2.finish_row()
    products(back_four, xr2, 0, SLOTS // 4)
    gather2.forward(2, 4)
    products(back_four, xr2, SLOTS // 4, SLOTS // 2)
    gather2.forward(4)
    early.start(1, early.finish(0))
    products(back_four, xr2, SLOTS // 2, SLOTS)
    col_part()
    relays = start_col_sum(1)
    early.start(2, early.finish(1))

    held = {}

    def first_inverses():
        grams = early.finish(2)
        g00 = symmetric(unpack(grams[0:8]))
        g01 = unpack(grams[8:16])
        g11 = symmetric(unpack(grams[16:24]))
        s01 = symmetric(g01)
        inv_curve = inverse(g00 - s01)
        inv_gram = inverse(g00)
        held["all"] = g00, g01, g11, s01, inv_curve, inv_gram

    def first_systems():
        g00, g01, g11, s01, inv_curve, inv_gram = held["all"]
        p1 = small_mm(g00, inv_curve)
        p0 = -small_mm(s01, inv_curve)
        p0_t, p1_t = flip(p0), flip(p1)
        newgram = small_mm(small_mm(p0, g00), p0_t) + small_mm(small_mm(p1, g11), p1_t)
        newgram = symmetric(newgram + 2.0 * small_mm(small_mm(p0, g01), p1_t))
        d0 = p0 + small_mm(newgram, inv_gram)
        direction = lanes(d0[:, 0:32], p1[:, 0:32])
        applied = lanes(d0[:, 0:32], p1[:, 0:32] - d0[:, 0:32], -p1[:, 0:32])
        whole = jnp.concatenate(
            [
                lanes(g00[:, 0:32], g01[:, 0:32], g11[:, 0:32]),
                lanes(flip(g01)[:, 0:32], g11[:, 0:32]),
            ],
            axis=0,
        )
        known = small_mm(direction, mm_high(whole, tall(applied).T))
        coef = jnp.concatenate([direction, lanes(p0[:, 0:32], p1[:, 0:32]), p1], axis=0)
        vectors[...] = mm_high(coef, basis[...])
        return newgram, p1, p1_t, applied, known

    gather2.finish_col()

    def add_share(g, total):
        for n in range(0, 2 * PS, 2):
            v = g * 2 * PS + n
            here = jnp.concatenate([xc2[v], xc2[v + 1]], axis=1)
            there = jnp.concatenate([out_cb[v], out_cb[v + 1]], axis=1)
            total = total + mm(here, there, True)
        return total

    share = lax.fori_loop(0, C // 2, add_share, jnp.zeros((32, 32), F32))
    late = Reduce(1, gram_l, gram_li)
    late.start(0, pack(WEIGHT * share))
    products(ahead_four, xc2, 0, SLOTS // 2)
    hand_on(1, relays)
    late.start(1, late.finish(0))
    products(ahead_four, xc2, SLOTS // 2, SLOTS)
    late.start(2, late.finish(1))
    first_inverses()
    row_part()
    start_row_sum(1)
    own = start_z_sum(1)
    newgram, p1, p1_t, applied, known = first_systems()
    g12 = symmetric(unpack(late.finish(2)))
    curve = symmetric(known - small_mm(small_mm(p1, g12), p1_t))
    steps = small_mm(newgram, inverse(curve))
    sol_ref[...] = vectors[64:96, :] + mm_high(steps, tall(vectors[0:32, :]))
    summed = finish_sums(1, own)
    scaling = scale[...]
    for p in range(PS):
        u2 = (0.5 * WEIGHT) * scaling[p : p + 1] * summed[p]
        basis[64:96, p * 128 : (p + 1) * 128] = u2
    image = mm_high(applied, basis[...])
    res_ref[...] = vectors[32:64, :] - mm_high(steps, tall(image))


def split_col(count):
    return (4, count // 4) if count >= 8 else (2, count // 2)


def solution(mesh):
    R, C = mesh.shape["row"], mesh.shape["col"]
    Y, Z = split_col(C)
    RB, CB = R * PS, C * PS

    def body(queries, block_spots, live_blocks, neighbor_cols, neighbor_sims):
        slots = block_spots.shape[2]
        vmem = pltpu.VMEM
        sems = pltpu.SemaphoreType.DMA
        ways = 2 if Y == 4 else 1
        scratch = [
            vmem(queries.shape, F32), vmem((1, slots), jnp.int32),
            vmem(neighbor_cols.shape[2:], jnp.int32), vmem(neighbor_sims.shape[2:], BF16),
            vmem((slots, 128, 128), BF16), vmem((slots, 128), F32), vmem((slots, 128), F32),
            vmem((128, PS * 128), F32), vmem((96, PS * 128), F32), vmem((PS, 128), F32),
            vmem((CB, 32, 128), BF16), vmem((RB, 32, 128), BF16),
            vmem((CB, 32, 128), BF16), vmem((RB, 32, 128), BF16),
            vmem((32, slots, 128), F32), vmem((32, slots, 128), F32),
            vmem((RB, 32, 128), F32), vmem((CB, 32, 128), F32),
            vmem((RB, 32, 128), BF16), vmem((CB, 32, 128), BF16),
            vmem((R, PS, 128), F32), vmem((C, PS, 128), F32),
            vmem((R, PS, 128), F32), vmem((C, PS, 128), F32),
            vmem((R, PS, 128), F32), vmem((C, PS, 128), F32),
            vmem((2, Z, ways, PS, 32, 128), BF16), vmem((2, Z, PS, 32, 128), BF16),
            vmem((2, Z, PS, 32, 128), BF16), vmem((2, Z, PS, 32, 128), BF16),
            vmem((2, Z, PS, 32, 128), BF16), vmem((2, R, PS, 32, 128), BF16),
            vmem((3, 24, 128), F32), vmem((3, max(R, Z, Y), 24, 128), F32),
            vmem((3, 8, 128), F32), vmem((3, max(R, Z, Y), 8, 128), F32),
            sems((10,)), sems((2, Z)), sems((2, 4)), sems((4,)), sems((4,)),
            sems((2, Z)), sems((2, Z)), sems((2, 5)), sems((2, 3, 2)),
        ]
        in_vmem = pl.BlockSpec(memory_space=pltpu.VMEM)
        in_any = pl.BlockSpec(memory_space=pl.ANY)
        in_smem = pl.BlockSpec(memory_space=pltpu.SMEM)
        shape = jax.ShapeDtypeStruct(queries.shape, F32)
        return pl.pallas_call(
            functools.partial(kernel, (R, Y, Z)),
            out_shape=(shape, shape),
            in_specs=[in_any, in_smem, in_any, in_smem, in_any, in_any],
            out_specs=(in_vmem, in_vmem),
            scratch_shapes=scratch,
            compiler_params=pltpu.CompilerParams(
                collective_id=0, has_side_effects=True, vmem_limit_bytes=53 * 1024 * 1024 + 512 * 1024
            ),
        )(
            queries,
            block_spots[0, 0],
            block_spots[0],
            live_blocks,
            neighbor_cols[0, 0],
            neighbor_sims[0, 0],
        )

    placed = (
        P(None, ("row", "col")),
        P("row", "col", None),
        P("row", "col"),
        P("row", "col", None, None, None),
        P("row", "col", None, None, None),
    )
    return jax.shard_map(
        body,
        mesh=mesh,
        in_specs=placed,
        out_specs=(P(None, ("row", "col")), P(None, ("row", "col"))),
        check_vma=False,
    )
```

```python
import functools

import jax
import jax.numpy as jnp
from jax import lax
from jax.experimental import pallas as pl
from jax.experimental.pallas import tpu as pltpu
from jax.sharding import PartitionSpec as P

MESH = pl.DeviceIdType.MESH
HIGH = lax.Precision.HIGHEST
F32 = jnp.float32
BF16 = jnp.bfloat16
WEIGHT = 0.95
PS = 4
UNROLL = 8
BUILD = 16


def mm(first, second, transposed=False):
    dims = (((1,), (1 if transposed else 0,)), ((), ()))
    return lax.dot_general(first, second, dims, preferred_element_type=F32)


def mm_high(first, second, transposed=False):
    dims = (((1,), (1 if transposed else 0,)), ((), ()))
    return lax.dot_general(first, second, dims, precision=HIGH, preferred_element_type=F32)


def lanes(*parts):
    width = sum(p.shape[1] for p in parts)
    return jnp.concatenate(list(parts) + [jnp.zeros((parts[0].shape[0], 128 - width), F32)], axis=1)


def tall(small):
    return jnp.concatenate([small, jnp.zeros((128 - small.shape[0], small.shape[1]), F32)], axis=0)


def pack(square):
    return jnp.concatenate([square[8 * i : 8 * i + 8, 0:32] for i in range(4)], axis=1)


def unpack(packed):
    return lanes(jnp.concatenate([packed[:, 32 * i : 32 * i + 32] for i in range(4)], axis=0))


def wait_all(ref, sem):
    pltpu.make_async_copy(ref, ref, sem).wait()


def flip(small):
    return tall(small).T[0:32]


def symmetric(small):
    return 0.5 * (small + flip(small))


def small_mm(first, second):
    return mm_high(first, tall(second))


def inverse(small):
    size = small.shape[0]
    row_ids = lax.broadcasted_iota(jnp.int32, small.shape, 0)
    lane_ids = lax.broadcasted_iota(jnp.int32, small.shape, 1)
    both = small + (row_ids + size == lane_ids).astype(F32)
    for k in range(size):
        pivot_row = both[k : k + 1, :] / both[k : k + 1, k : k + 1]
        both = jnp.where(row_ids == k, pivot_row, both - both[:, k : k + 1] * pivot_row)
    return lanes(both[:, size : 2 * size])


def kernel(
    sizes, q_hbm, spots_ref, spot_row_hbm, live_ref, cols_hbm, sims_hbm, sol_ref, res_ref,
    q_ref, spot_row_ref, cols_ref, sims_ref, blocks, colsum, rowsum, basis, vectors, scale,
    xc, xr, xc2, xr2, fwd, bwd, out_r, out_c, out_rb, out_cb,
    deg_r, deg_c, deg_rr, deg_cr, scl_r, scl_c,
    yr, relay_in, relay_out, zs, zr, rr, gram_e, gram_ei, gram_l, gram_li,
    in_s, ag_z, ag_sem, dg_sem, sc_sem, rs_relay, rs_y, rs_sem, ar_sem,
):
    R, Y, Z = sizes
    C = Y * Z
    RB, CB = R * PS, C * PS
    SLOTS = blocks.shape[0]
    shift = CB.bit_length() - 1
    a = lax.axis_index("row")
    b = lax.axis_index("col")
    y = b // Z
    z = b % Z

    def row_dev(k):
        return (lax.rem(a + k, R), b)

    def col_dev(k):
        return (a, lax.rem(b + k, C))

    def z_dev(k):
        return (a, y * Z + lax.rem(z + k, Z))

    def y_dev(k):
        return (a, lax.rem(y + k, Y) * Z + z)

    def copy(src, dst, ss, rs, dev):
        return pltpu.make_async_remote_copy(
            src_ref=src, dst_ref=dst, send_sem=ss, recv_sem=rs, device_id=dev, device_id_type=MESH
        )

    barrier = pltpu.get_barrier_semaphore()
    for k in range(1, R):
        pl.semaphore_signal(barrier, inc=1, device_id=row_dev(k), device_id_type=MESH)
    for k in range(1, C):
        pl.semaphore_signal(barrier, inc=1, device_id=col_dev(k), device_id_type=MESH)

    quarter = SLOTS // 4
    loads = []
    for n in range(4):
        part = pl.ds(n * quarter, quarter)
        loads.append(
            (
                pltpu.make_async_copy(cols_hbm.at[part], cols_ref.at[part], in_s.at[n]),
                pltpu.make_async_copy(sims_hbm.at[part], sims_ref.at[part], in_s.at[4 + n]),
            )
        )
    others = (
        pltpu.make_async_copy(q_hbm, q_ref, in_s.at[8]),
        pltpu.make_async_copy(spot_row_hbm, spot_row_ref, in_s.at[9]),
    )
    for c in [*others, *loads[0], *loads[1], *loads[2], *loads[3]]:
        c.start()

    near_first = sorted(range(1, Z), key=lambda k: (min(k, Z - k), k))

    class Gather:
        def __init__(self, turn, col_buf, row_buf):
            self.turn, self.col_buf, self.row_buf = turn, col_buf, row_buf
            mine_c = col_buf.at[pl.ds(b * PS, PS)]
            mine_r = row_buf.at[pl.ds(a * PS, PS)]
            col_sent, row_sent, y_got, row_got = [ag_sem.at[turn, n] for n in range(4)]
            self.row = [copy(mine_r, mine_r, row_sent, row_got, row_dev(k)) for k in range(1, R)]
            self.z = {k: copy(mine_c, mine_c, col_sent, ag_z.at[turn, k], z_dev(k)) for k in range(1, Z)}
            self.y = {}
            for kz in range(Z):
                chunk = col_buf.at[pl.ds((y * Z + lax.rem(z - kz + Z, Z)) * PS, PS)]
                self.y[kz] = [
                    copy(chunk, chunk, col_sent, y_got, y_dev(ky)) for ky in ((2, 1, 3) if Y == 4 else (1,))
                ]

        def start(self):
            for c in self.y[0]:
                c.start()
            for kz in near_first:
                self.z[kz].start()
            for c in self.row:
                c.start()

        def forward(self, first=0, last=None):
            for kz in near_first[first:last]:
                self.z[kz].wait_recv()
                for c in self.y[kz]:
                    c.start()

        def finish_row(self):
            wait_all(self.row_buf.at[pl.ds(0, (R - 1) * PS)], ag_sem.at[self.turn, 3])
            wait_all(self.row_buf.at[pl.ds(0, (R - 1) * PS)], ag_sem.at[self.turn, 1])

        def finish_col(self):
            wait_all(self.col_buf.at[pl.ds(0, (Y - 1) * Z * PS)], ag_sem.at[self.turn, 2])
            wait_all(self.col_buf.at[pl.ds(0, (C - 1) * PS)], ag_sem.at[self.turn, 0])

    gather1 = Gather(0, xc, xr)

    lane_ids = lax.broadcasted_iota(jnp.int32, (128, 128), 0).astype(jnp.int16)
    halves = (
        lax.broadcasted_iota(jnp.int32, (8, 256), 0)
        == lax.shift_right_logical(lax.broadcasted_iota(jnp.int32, (8, 256), 1), 7)
    )
    halves = jnp.where(halves, 1.0, 0.0).astype(BF16)

    def build(s):
        idx = cols_ref[s]
        sim = sims_ref[s].astype(F32)
        value = jnp.zeros(sim.shape, F32)
        for t in range(idx.shape[0]):
            value = value + jnp.where(idx == idx[t : t + 1], sim[t : t + 1], 0.0)
        value = value.astype(BF16)
        idx = idx.astype(jnp.int16)
        block = jnp.zeros((128, 128), BF16)
        for t in range(idx.shape[0]):
            here = lane_ids == jnp.broadcast_to(idx[t : t + 1], (128, 128))
            block = jnp.where(here, jnp.broadcast_to(value[t : t + 1], (128, 128)), block)
        blocks[s] = block
        rowsum[pl.ds(s, 1), :] = jnp.sum(sim, axis=0, keepdims=True)
        return block

    def build_turn(g, carry):
        turns = SLOTS // BUILD
        for n in range(4):

            @pl.when(g == n * turns // 4)
            def _():
                for c in loads[n]:
                    c.wait()

        @pl.when(g == turns // 2)
        def _():
            gather1.forward()

        for u in range(0, BUILD, 4):
            s = g * BUILD + u
            four = [build(s + v) for v in range(4)]
            pairs = jnp.concatenate(
                [jnp.concatenate([four[0], four[2]], 1), jnp.concatenate([four[1], four[3]], 1)], 0
            )
            sums = mm(halves, pairs, True)
            colsum[pl.ds(s, 1), :] = sums[0:1, 0:128]
            colsum[pl.ds(s + 1, 1), :] = sums[0:1, 128:256]
            colsum[pl.ds(s + 2, 1), :] = sums[1:2, 0:128]
            colsum[pl.ds(s + 3, 1), :] = sums[1:2, 128:256]
        return carry

    for c in others:
        c.wait()
    basis[32:128, :] = jnp.zeros((96, PS * 128), F32)
    for p in range(PS):
        part = q_ref[:, p * 128 : (p + 1) * 128]
        basis[0:32, p * 128 : (p + 1) * 128] = part
        xc[b * PS + p] = part.astype(BF16)
        xr[a * PS + p] = part.astype(BF16)
    pl.semaphore_wait(barrier, R - 1 + C - 1)
    gather1.start()
    lax.fori_loop(0, SLOTS // BUILD, build_turn, 0)

    spot_row = spot_row_ref[...]
    live = live_ref[0, 0]
    used = lax.broadcasted_iota(jnp.int32, (1, SLOTS), 1) < live
    in_row = (lax.shift_right_logical(spot_row, shift) == lax.broadcasted_iota(jnp.int32, (RB, SLOTS), 0)) & used
    in_col = ((spot_row & (CB - 1)) == lax.broadcasted_iota(jnp.int32, (CB, SLOTS), 0)) & used
    in_row_f = jnp.where(in_row, 1.0, 0.0).astype(F32)
    in_col_f = jnp.where(in_col, 1.0, 0.0).astype(F32)
    row_degree = mm_high(in_row_f, rowsum[...])
    col_degree = mm_high(in_col_f, colsum[...])
    for g in range(R):
        deg_r[g] = row_degree[g * PS : (g + 1) * PS]
    for g in range(C):
        deg_c[g] = col_degree[g * PS : (g + 1) * PS]
    for k in range(1, C):
        copy(deg_c.at[lax.rem(b + k, C)], deg_cr.at[k], dg_sem.at[0], dg_sem.at[1], col_dev(k)).start()
    for k in range(1, R):
        copy(deg_r.at[lax.rem(a + k, R)], deg_rr.at[k], dg_sem.at[2], dg_sem.at[3], row_dev(k)).start()
    degree = deg_r[a] + deg_c[b]
    wait_all(deg_rr.at[pl.ds(1, R - 1)], dg_sem.at[3])
    wait_all(deg_cr.at[pl.ds(1, C - 1)], dg_sem.at[1])
    for k in range(1, C):
        degree = degree + deg_cr[k]
    for k in range(1, R):
        degree = degree + deg_rr[k]
    degree = 1.0 + 0.5 * degree
    scaling = 1.0 / jnp.sqrt(degree)
    scl_r[a] = scaling
    scl_c[b] = scaling
    scale[...] = scaling
    for k in range(1, R):
        copy(scl_r.at[a], scl_r.at[a], sc_sem.at[2], sc_sem.at[3], row_dev(k)).start()
    for k in range(1, C):
        copy(scl_c.at[b], scl_c.at[b], sc_sem.at[0], sc_sem.at[1], col_dev(k)).start()
    gather1.finish_row()
    wait_all(deg_rr.at[pl.ds(1, R - 1)], dg_sem.at[2])
    wait_all(deg_cr.at[pl.ds(1, C - 1)], dg_sem.at[0])
    for n in range(2):
        wait_all(scl_r.at[pl.ds(0, R - 1)], sc_sem.at[2 + n])

    def scale_part(buf, scl, g):
        factors = scl[g]
        for p in range(PS):
            buf[g * PS + p] = (buf[g * PS + p].astype(F32) * factors[p : p + 1]).astype(BF16)

    def scale_cols(g, carry):
        scale_part(xc, scl_c, g)
        return carry

    def scale_rows(g, carry):
        scale_part(xr, scl_r, g)
        return carry

    lax.fori_loop(0, R, scale_rows, 0)

    def spread(x):
        zero = jnp.zeros((32, 128), BF16)
        pairs = [(x[0], zero), (x[1], zero), (zero, x[2]), (zero, x[3])]
        return jnp.concatenate([jnp.concatenate(pair, 1) for pair in pairs], 0)

    def square(x):
        return jnp.concatenate([jnp.concatenate(x[0:2], 1), jnp.concatenate(x[2:4], 1)], 0)

    def back_four(s, row_buf):
        x = [row_buf[lax.shift_right_logical(spots_ref[s + n], shift)] for n in range(4)]
        out = mm(spread(x), square([blocks[s], blocks[s + 2], blocks[s + 1], blocks[s + 3]]), True)
        for n in range(4):
            bwd[:, s + n, :] = out[32 * n : 32 * n + 32, 128 * (n & 1) : 128 * (n & 1) + 128]

    def ahead_four(s, col_buf):
        x = [col_buf[spots_ref[s + n] & (CB - 1)] for n in range(4)]
        out = mm(spread(x), square([blocks[s + n] for n in range(4)]))
        for n in range(4):
            fwd[:, s + n, :] = out[32 * n : 32 * n + 32, 128 * (n & 1) : 128 * (n & 1) + 128]

    def products(four, buf, low, high):
        def turn(g, carry):
            for u in range(UNROLL):
                four((g * UNROLL + u) * 4, buf)
            return carry

        lax.fori_loop(low // (4 * UNROLL), high // (4 * UNROLL), turn, 0)

    pick_r = in_row_f.astype(BF16)
    pick_c = in_col_f.astype(BF16)

    def gather_sum(pick, terms):
        return mm(pick, terms.astype(BF16))

    def col_part():
        for m in range(32):
            out_c[:, m, :] = gather_sum(pick_c, bwd[m])

        def to_wire(v, carry):
            for p in range(2 * PS):
                out_cb[v * 2 * PS + p] = out_c[v * 2 * PS + p].astype(BF16)
            return carry

        lax.fori_loop(0, C // 2, to_wire, 0)

    def row_part():
        for m in range(32):
            out_r[:, m, :] = gather_sum(pick_r, fwd[m])
        for v in range(RB):
            out_rb[v] = out_r[v].astype(BF16)

    ways = (1, Y - 1) if Y == 4 else (1,)

    def relay_way(kz):
        return 0 if kz % 2 == 0 else 1

    places = [lax.rem(z + kz, Z) for kz in range(Z)]
    order = list(reversed(near_first)) + [0]

    def target(ky, kz):
        return pl.ds((lax.rem(y + ky, Y) * Z + places[kz]) * PS, PS)

    def half(turn, src, kz, w):
        copy(src, yr.at[turn, kz, w], rs_sem.at[turn, 0], rs_y.at[turn, kz], y_dev(ways[w])).start()

    def start_col_sum(turn):
        relays = {}
        if Y == 4:
            for kz in order:
                relays[kz] = copy(
                    out_cb.at[target(2, kz)],
                    relay_in.at[turn, kz],
                    rs_sem.at[turn, 0],
                    rs_relay.at[turn, kz],
                    y_dev(ways[relay_way(kz)]),
                )
                relays[kz].start()
        for kz in order:
            for w, ky in enumerate(ways):
                if Y != 4 or w != relay_way(kz):
                    half(turn, out_cb.at[target(ky, kz)], kz, w)
        return relays

    def start_row_sum(turn):
        for k in range(1, R):
            src = out_rb.at[pl.ds(lax.rem(a + k, R) * PS, PS)]
            copy(src, rr.at[turn, k], rs_sem.at[turn, 3], rs_sem.at[turn, 4], row_dev(k)).start()

    def hand_on(turn, relays):
        for kz in relays:
            w = relay_way(kz)
            relays[kz].wait_recv()
            total = out_c[target(ways[w], kz)] + relay_in[turn, kz].astype(F32)
            relay_out[turn, kz] = total.astype(BF16)
            half(turn, relay_out.at[turn, kz], kz, w)

    def start_z_sum(turn):
        for kz in order:
            total = out_c[target(0, kz)]
            wait_all(yr.at[turn, kz], rs_y.at[turn, kz])
            for w in range(len(ways)):
                total = total + yr[turn, kz, w].astype(F32)
            if kz:
                zs[turn, kz] = total.astype(BF16)
                copy(
                    zs.at[turn, kz], zr.at[turn, kz], rs_sem.at[turn, 1], rs_sem.at[turn, 2], z_dev(kz)
                ).start()
        return total

    def finish_sums(turn, own):
        y_sent, z_sent, z_got, row_sent, row_got = [rs_sem.at[turn, n] for n in range(5)]
        own = own + out_r[pl.ds(a * PS, PS)]
        wait_all(zr.at[turn, pl.ds(1, Z - 1)], z_got)
        for kz in range(1, Z):
            own = own + zr[turn, kz].astype(F32)
        wait_all(rr.at[turn, pl.ds(1, R - 1)], row_got)
        for k in range(1, R):
            own = own + rr[turn, k].astype(F32)
        wait_all(out_cb.at[pl.ds(0, (Y - 1) * Z * PS)], y_sent)
        wait_all(rr.at[turn, pl.ds(1, R - 1)], row_sent)
        wait_all(zr.at[turn, pl.ds(1, Z - 1)], z_sent)
        return own

    class Reduce:
        def __init__(self, turn, buf, buf_in):
            self.turn, self.buf, self.buf_in = turn, buf, buf_in

        def start(self, stage, value):
            count, dev = ((R, row_dev), (Z, z_dev), (Y, y_dev))[stage]
            self.buf[stage] = value
            for k in range(1, count):
                copy(
                    self.buf.at[stage],
                    self.buf_in.at[stage, k],
                    ar_sem.at[self.turn, stage, 0],
                    ar_sem.at[self.turn, stage, 1],
                    dev(k),
                ).start()

        def finish(self, stage):
            count = (R, Z, Y)[stage]
            there = self.buf_in.at[stage, pl.ds(1, count - 1)]
            wait_all(there, ar_sem.at[self.turn, stage, 1])
            total = self.buf[stage]
            for k in range(1, count):
                total = total + self.buf_in[stage, k]
            wait_all(there, ar_sem.at[self.turn, stage, 0])
            return total

    products(back_four, xr, 0, SLOTS)
    col_part()
    relays = start_col_sum(0)
    for n in range(2):
        wait_all(scl_c.at[pl.ds(0, C - 1)], sc_sem.at[n])
    gather1.finish_col()
    lax.fori_loop(0, C, scale_cols, 0)
    products(ahead_four, xc, 0, SLOTS // 2)
    hand_on(0, relays)
    products(ahead_four, xc, SLOTS // 2, SLOTS)
    row_part()
    start_row_sum(0)
    summed = finish_sums(0, start_z_sum(0))
    scaling = scale[...]
    for p in range(PS):
        u1 = (0.5 * WEIGHT) * scaling[p : p + 1] * summed[p]
        basis[32:64, p * 128 : (p + 1) * 128] = u1
        part = (scaling[p : p + 1] * u1).astype(BF16)
        xc2[b * PS + p] = part
        xr2[a * PS + p] = part
    gather2 = Gather(1, xc2, xr2)
    gather2.start()
    early = Reduce(0, gram_e, gram_ei)
    g0 = mm_high(basis[0:64, :], basis[0:64, :], True)
    early.start(
        0, jnp.concatenate([pack(g0[0:32]), pack(g0[0:32, 32:64]), pack(g0[32:64, 32:64])], axis=0)
    )
    gather2.forward(0, 2)
    gather2.finish_row()
    products(back_four, xr2, 0, SLOTS // 4)
    gather2.forward(2, 4)
    products(back_four, xr2, SLOTS // 4, SLOTS // 2)
    gather2.forward(4)
    early.start(1, early.finish(0))
    products(back_four, xr2, SLOTS // 2, SLOTS)
    col_part()
    relays = start_col_sum(1)
    early.start(2, early.finish(1))

    held = {}

    def first_inverses():
        grams = early.finish(2)
        g00 = symmetric(unpack(grams[0:8]))
        g01 = unpack(grams[8:16])
        g11 = symmetric(unpack(grams[16:24]))
        s01 = symmetric(g01)
        inv_curve = inverse(g00 - s01)
        inv_gram = inverse(g00)
        held["all"] = g00, g01, g11, s01, inv_curve, inv_gram

    def first_systems():
        g00, g01, g11, s01, inv_curve, inv_gram = held["all"]
        p1 = small_mm(g00, inv_curve)
        p0 = -small_mm(s01, inv_curve)
        p0_t, p1_t = flip(p0), flip(p1)
        newgram = small_mm(small_mm(p0, g00), p0_t) + small_mm(small_mm(p1, g11), p1_t)
        newgram = symmetric(newgram + 2.0 * small_mm(small_mm(p0, g01), p1_t))
        d0 = p0 + small_mm(newgram, inv_gram)
        direction = lanes(d0[:, 0:32], p1[:, 0:32])
        applied = lanes(d0[:, 0:32], p1[:, 0:32] - d0[:, 0:32], -p1[:, 0:32])
        whole = jnp.concatenate(
            [
                lanes(g00[:, 0:32], g01[:, 0:32], g11[:, 0:32]),
                lanes(flip(g01)[:, 0:32], g11[:, 0:32]),
            ],
            axis=0,
        )
        known = small_mm(direction, mm_high(whole, tall(applied).T))
        coef = jnp.concatenate([direction, lanes(p0[:, 0:32], p1[:, 0:32]), p1], axis=0)
        vectors[...] = mm_high(coef, basis[...])
        return newgram, p1, p1_t, applied, known

    gather2.finish_col()

    def add_share(g, total):
        for n in range(0, 2 * PS, 2):
            v = g * 2 * PS + n
            here = jnp.concatenate([xc2[v], xc2[v + 1]], axis=1)
            there = jnp.concatenate([out_cb[v], out_cb[v + 1]], axis=1)
            total = total + mm(here, there, True)
        return total

    share = lax.fori_loop(0, C // 2, add_share, jnp.zeros((32, 32), F32))
    late = Reduce(1, gram_l, gram_li)
    late.start(0, pack(WEIGHT * share))
    products(ahead_four, xc2, 0, SLOTS // 2)
    hand_on(1, relays)
    late.start(1, late.finish(0))
    products(ahead_four, xc2, SLOTS // 2, SLOTS)
    late.start(2, late.finish(1))
    first_inverses()
    row_part()
    start_row_sum(1)
    own = start_z_sum(1)
    newgram, p1, p1_t, applied, known = first_systems()
    g12 = symmetric(unpack(late.finish(2)))
    curve = symmetric(known - small_mm(small_mm(p1, g12), p1_t))
    steps = small_mm(newgram, inverse(curve))
    sol_ref[...] = vectors[64:96, :] + mm_high(steps, tall(vectors[0:32, :]))
    summed = finish_sums(1, own)
    scaling = scale[...]
    for p in range(PS):
        u2 = (0.5 * WEIGHT) * scaling[p : p + 1] * summed[p]
        basis[64:96, p * 128 : (p + 1) * 128] = u2
    image = mm_high(applied, basis[...])
    res_ref[...] = vectors[32:64, :] - mm_high(steps, tall(image))


def split_col(count):
    return (4, count // 4) if count >= 8 else (2, count // 2)


def solution(mesh):
    R, C = mesh.shape["row"], mesh.shape["col"]
    Y, Z = split_col(C)
    RB, CB = R * PS, C * PS

    def body(queries, block_spots, live_blocks, neighbor_cols, neighbor_sims):
        slots = block_spots.shape[2]
        vmem = pltpu.VMEM
        sems = pltpu.SemaphoreType.DMA
        ways = 2 if Y == 4 else 1
        scratch = [
            vmem(queries.shape, F32), vmem((1, slots), jnp.int32),
            vmem(neighbor_cols.shape[2:], jnp.int32), vmem(neighbor_sims.shape[2:], BF16),
            vmem((slots, 128, 128), BF16), vmem((slots, 128), F32), vmem((slots, 128), F32),
            vmem((128, PS * 128), F32), vmem((96, PS * 128), F32), vmem((PS, 128), F32),
            vmem((CB, 32, 128), BF16), vmem((RB, 32, 128), BF16),
            vmem((CB, 32, 128), BF16), vmem((RB, 32, 128), BF16),
            vmem((32, slots, 128), F32), vmem((32, slots, 128), F32),
            vmem((RB, 32, 128), F32), vmem((CB, 32, 128), F32),
            vmem((RB, 32, 128), BF16), vmem((CB, 32, 128), BF16),
            vmem((R, PS, 128), F32), vmem((C, PS, 128), F32),
            vmem((R, PS, 128), F32), vmem((C, PS, 128), F32),
            vmem((R, PS, 128), F32), vmem((C, PS, 128), F32),
            vmem((2, Z, ways, PS, 32, 128), BF16), vmem((2, Z, PS, 32, 128), BF16),
            vmem((2, Z, PS, 32, 128), BF16), vmem((2, Z, PS, 32, 128), BF16),
            vmem((2, Z, PS, 32, 128), BF16), vmem((2, R, PS, 32, 128), BF16),
            vmem((3, 24, 128), F32), vmem((3, max(R, Z, Y), 24, 128), F32),
            vmem((3, 8, 128), F32), vmem((3, max(R, Z, Y), 8, 128), F32),
            sems((10,)), sems((2, Z)), sems((2, 4)), sems((4,)), sems((4,)),
            sems((2, Z)), sems((2, Z)), sems((2, 5)), sems((2, 3, 2)),
        ]
        in_vmem = pl.BlockSpec(memory_space=pltpu.VMEM)
        in_any = pl.BlockSpec(memory_space=pl.ANY)
        in_smem = pl.BlockSpec(memory_space=pltpu.SMEM)
        shape = jax.ShapeDtypeStruct(queries.shape, F32)
        return pl.pallas_call(
            functools.partial(kernel, (R, Y, Z)),
            out_shape=(shape, shape),
            in_specs=[in_any, in_smem, in_any, in_smem, in_any, in_any],
            out_specs=(in_vmem, in_vmem),
            scratch_shapes=scratch,
            compiler_params=pltpu.CompilerParams(
                collective_id=0, has_side_effects=True, vmem_limit_bytes=53 * 1024 * 1024 + 512 * 1024
            ),
        )(
            queries,
            block_spots[0, 0],
            block_spots[0],
            live_blocks,
            neighbor_cols[0, 0],
            neighbor_sims[0, 0],
        )

    placed = (
        P(None, ("row", "col")),
        P("row", "col", None),
        P("row", "col"),
        P("row", "col", None, None, None),
        P("row", "col", None, None, None),
    )
    return jax.shard_map(
        body,
        mesh=mesh,
        in_specs=placed,
        out_specs=(P(None, ("row", "col")), P(None, ("row", "col"))),
        check_vma=False,
    )
```

```python
import functools

import jax
import jax.numpy as jnp
from jax import lax
from jax.experimental import pallas as pl
from jax.experimental.pallas import tpu as pltpu
from jax.sharding import PartitionSpec as P

MESH = pl.DeviceIdType.MESH
HIGH = lax.Precision.HIGHEST
F32 = jnp.float32
BF16 = jnp.bfloat16
WEIGHT = 0.95
PS = 4
UNROLL = 8
BUILD = 32


def mm(first, second, transposed=False):
    dims = (((1,), (1 if transposed else 0,)), ((), ()))
    return lax.dot_general(first, second, dims, preferred_element_type=F32)


def mm_high(first, second, transposed=False):
    dims = (((1,), (1 if transposed else 0,)), ((), ()))
    return lax.dot_general(first, second, dims, precision=HIGH, preferred_element_type=F32)


def lanes(*parts):
    width = sum(p.shape[1] for p in parts)
    return jnp.concatenate(list(parts) + [jnp.zeros((parts[0].shape[0], 128 - width), F32)], axis=1)


def tall(small):
    return jnp.concatenate([small, jnp.zeros((128 - small.shape[0], small.shape[1]), F32)], axis=0)


def pack(square):
    return jnp.concatenate([square[8 * i : 8 * i + 8, 0:32] for i in range(4)], axis=1)


def unpack(packed):
    return lanes(jnp.concatenate([packed[:, 32 * i : 32 * i + 32] for i in range(4)], axis=0))


def wait_all(ref, sem):
    pltpu.make_async_copy(ref, ref, sem).wait()


def flip(small):
    return tall(small).T[0:32]


def symmetric(small):
    return 0.5 * (small + flip(small))


def small_mm(first, second):
    return mm_high(first, tall(second))


def inverse(small):
    size = small.shape[0]
    row_ids = lax.broadcasted_iota(jnp.int32, small.shape, 0)
    lane_ids = lax.broadcasted_iota(jnp.int32, small.shape, 1)
    both = small + (row_ids + size == lane_ids).astype(F32)
    for k in range(size):
        pivot_row = both[k : k + 1, :] / both[k : k + 1, k : k + 1]
        both = jnp.where(row_ids == k, pivot_row, both - both[:, k : k + 1] * pivot_row)
    return lanes(both[:, size : 2 * size])


def kernel(
    sizes, q_hbm, spots_ref, spot_row_hbm, live_ref, cols_hbm, sims_hbm, sol_ref, res_ref,
    q_ref, spot_row_ref, cols_ref, sims_ref, blocks, colsum, rowsum, basis, vectors, scale,
    xc, xr, xc2, xr2, fwd, bwd, out_r, out_c, out_rb, out_cb,
    deg_r, deg_c, deg_rr, deg_cr, scl_r, scl_c,
    yr, relay_in, relay_out, zs, zr, rr, gram_e, gram_ei, gram_l, gram_li,
    in_s, ag_z, ag_sem, dg_sem, sc_sem, rs_relay, rs_y, rs_sem, ar_sem,
):
    R, Y, Z = sizes
    C = Y * Z
    RB, CB = R * PS, C * PS
    SLOTS = blocks.shape[0]
    shift = CB.bit_length() - 1
    a = lax.axis_index("row")
    b = lax.axis_index("col")
    y = b // Z
    z = b % Z

    def row_dev(k):
        return (lax.rem(a + k, R), b)

    def col_dev(k):
        return (a, lax.rem(b + k, C))

    def z_dev(k):
        return (a, y * Z + lax.rem(z + k, Z))

    def y_dev(k):
        return (a, lax.rem(y + k, Y) * Z + z)

    def copy(src, dst, ss, rs, dev):
        return pltpu.make_async_remote_copy(
            src_ref=src, dst_ref=dst, send_sem=ss, recv_sem=rs, device_id=dev, device_id_type=MESH
        )

    barrier = pltpu.get_barrier_semaphore()
    for k in range(1, R):
        pl.semaphore_signal(barrier, inc=1, device_id=row_dev(k), device_id_type=MESH)
    for k in range(1, C):
        pl.semaphore_signal(barrier, inc=1, device_id=col_dev(k), device_id_type=MESH)

    quarter = SLOTS // 4
    loads = []
    for n in range(4):
        part = pl.ds(n * quarter, quarter)
        loads.append(
            (
                pltpu.make_async_copy(cols_hbm.at[part], cols_ref.at[part], in_s.at[n]),
                pltpu.make_async_copy(sims_hbm.at[part], sims_ref.at[part], in_s.at[4 + n]),
            )
        )
    others = (
        pltpu.make_async_copy(q_hbm, q_ref, in_s.at[8]),
        pltpu.make_async_copy(spot_row_hbm, spot_row_ref, in_s.at[9]),
    )
    for c in [*others, *loads[0], *loads[1], *loads[2], *loads[3]]:
        c.start()

    near_first = sorted(range(1, Z), key=lambda k: (min(k, Z - k), k))

    class Gather:
        def __init__(self, turn, col_buf, row_buf):
            self.turn, self.col_buf, self.row_buf = turn, col_buf, row_buf
            mine_c = col_buf.at[pl.ds(b * PS, PS)]
            mine_r = row_buf.at[pl.ds(a * PS, PS)]
            col_sent, row_sent, y_got, row_got = [ag_sem.at[turn, n] for n in range(4)]
            self.row = [copy(mine_r, mine_r, row_sent, row_got, row_dev(k)) for k in range(1, R)]
            self.z = {k: copy(mine_c, mine_c, col_sent, ag_z.at[turn, k], z_dev(k)) for k in range(1, Z)}
            self.y = {}
            for kz in range(Z):
                chunk = col_buf.at[pl.ds((y * Z + lax.rem(z - kz + Z, Z)) * PS, PS)]
                self.y[kz] = [
                    copy(chunk, chunk, col_sent, y_got, y_dev(ky)) for ky in ((2, 1, 3) if Y == 4 else (1,))
                ]

        def start(self):
            for c in self.y[0]:
                c.start()
            for kz in near_first:
                self.z[kz].start()
            for c in self.row:
                c.start()

        def forward(self, first=0, last=None):
            for kz in near_first[first:last]:
                self.z[kz].wait_recv()
                for c in self.y[kz]:
                    c.start()

        def finish_row(self):
            wait_all(self.row_buf.at[pl.ds(0, (R - 1) * PS)], ag_sem.at[self.turn, 3])
            wait_all(self.row_buf.at[pl.ds(0, (R - 1) * PS)], ag_sem.at[self.turn, 1])

        def finish_col(self):
            wait_all(self.col_buf.at[pl.ds(0, (Y - 1) * Z * PS)], ag_sem.at[self.turn, 2])
            wait_all(self.col_buf.at[pl.ds(0, (C - 1) * PS)], ag_sem.at[self.turn, 0])

    gather1 = Gather(0, xc, xr)

    lane_ids = lax.broadcasted_iota(jnp.int32, (128, 128), 0).astype(jnp.int16)
    halves = (
        lax.broadcasted_iota(jnp.int32, (8, 256), 0)
        == lax.shift_right_logical(lax.broadcasted_iota(jnp.int32, (8, 256), 1), 7)
    )
    halves = jnp.where(halves, 1.0, 0.0).astype(BF16)

    def build(s):
        idx = cols_ref[s]
        sim = sims_ref[s].astype(F32)
        value = jnp.zeros(sim.shape, F32)
        for t in range(idx.shape[0]):
            value = value + jnp.where(idx == idx[t : t + 1], sim[t : t + 1], 0.0)
        value = value.astype(BF16)
        idx = idx.astype(jnp.int16)
        block = jnp.zeros((128, 128), BF16)
        for t in range(idx.shape[0]):
            here = lane_ids == jnp.broadcast_to(idx[t : t + 1], (128, 128))
            block = jnp.where(here, jnp.broadcast_to(value[t : t + 1], (128, 128)), block)
        blocks[s] = block
        rowsum[pl.ds(s, 1), :] = jnp.sum(sim, axis=0, keepdims=True)
        return block

    def build_turn(g, carry):
        turns = SLOTS // BUILD
        for n in range(4):

            @pl.when(g == n * turns // 4)
            def _():
                for c in loads[n]:
                    c.wait()

        @pl.when(g == turns // 2)
        def _():
            gather1.forward()

        for u in range(0, BUILD, 4):
            s = g * BUILD + u
            four = [build(s + v) for v in range(4)]
            pairs = jnp.concatenate(
                [jnp.concatenate([four[0], four[2]], 1), jnp.concatenate([four[1], four[3]], 1)], 0
            )
            sums = mm(halves, pairs, True)
            colsum[pl.ds(s, 1), :] = sums[0:1, 0:128]
            colsum[pl.ds(s + 1, 1), :] = sums[0:1, 128:256]
            colsum[pl.ds(s + 2, 1), :] = sums[1:2, 0:128]
            colsum[pl.ds(s + 3, 1), :] = sums[1:2, 128:256]
        return carry

    for c in others:
        c.wait()
    basis[32:128, :] = jnp.zeros((96, PS * 128), F32)
    for p in range(PS):
        part = q_ref[:, p * 128 : (p + 1) * 128]
        basis[0:32, p * 128 : (p + 1) * 128] = part
        xc[b * PS + p] = part.astype(BF16)
        xr[a * PS + p] = part.astype(BF16)
    pl.semaphore_wait(barrier, R - 1 + C - 1)
    gather1.start()
    lax.fori_loop(0, SLOTS // BUILD, build_turn, 0)

    spot_row = spot_row_ref[...]
    live = live_ref[0, 0]
    used = lax.broadcasted_iota(jnp.int32, (1, SLOTS), 1) < live
    in_row = (lax.shift_right_logical(spot_row, shift) == lax.broadcasted_iota(jnp.int32, (RB, SLOTS), 0)) & used
    in_col = ((spot_row & (CB - 1)) == lax.broadcasted_iota(jnp.int32, (CB, SLOTS), 0)) & used
    in_row_f = jnp.where(in_row, 1.0, 0.0).astype(F32)
    in_col_f = jnp.where(in_col, 1.0, 0.0).astype(F32)
    row_degree = mm_high(in_row_f, rowsum[...])
    col_degree = mm_high(in_col_f, colsum[...])
    for g in range(R):
        deg_r[g] = row_degree[g * PS : (g + 1) * PS]
    for g in range(C):
        deg_c[g] = col_degree[g * PS : (g + 1) * PS]
    for k in range(1, C):
        copy(deg_c.at[lax.rem(b + k, C)], deg_cr.at[k], dg_sem.at[0], dg_sem.at[1], col_dev(k)).start()
    for k in range(1, R):
        copy(deg_r.at[lax.rem(a + k, R)], deg_rr.at[k], dg_sem.at[2], dg_sem.at[3], row_dev(k)).start()
    degree = deg_r[a] + deg_c[b]
    wait_all(deg_rr.at[pl.ds(1, R - 1)], dg_sem.at[3])
    wait_all(deg_cr.at[pl.ds(1, C - 1)], dg_sem.at[1])
    for k in range(1, C):
        degree = degree + deg_cr[k]
    for k in range(1, R):
        degree = degree + deg_rr[k]
    degree = 1.0 + 0.5 * degree
    scaling = 1.0 / jnp.sqrt(degree)
    scl_r[a] = scaling
    scl_c[b] = scaling
    scale[...] = scaling
    for k in range(1, R):
        copy(scl_r.at[a], scl_r.at[a], sc_sem.at[2], sc_sem.at[3], row_dev(k)).start()
    for k in range(1, C):
        copy(scl_c.at[b], scl_c.at[b], sc_sem.at[0], sc_sem.at[1], col_dev(k)).start()
    gather1.finish_row()
    wait_all(deg_rr.at[pl.ds(1, R - 1)], dg_sem.at[2])
    wait_all(deg_cr.at[pl.ds(1, C - 1)], dg_sem.at[0])
    for n in range(2):
        wait_all(scl_r.at[pl.ds(0, R - 1)], sc_sem.at[2 + n])

    def scale_part(buf, scl, g):
        factors = scl[g]
        for p in range(PS):
            buf[g * PS + p] = (buf[g * PS + p].astype(F32) * factors[p : p + 1]).astype(BF16)

    def scale_cols(g, carry):
        scale_part(xc, scl_c, g)
        return carry

    def scale_rows(g, carry):
        scale_part(xr, scl_r, g)
        return carry

    lax.fori_loop(0, R, scale_rows, 0)

    def spread(x):
        zero = jnp.zeros((32, 128), BF16)
        pairs = [(x[0], zero), (x[1], zero), (zero, x[2]), (zero, x[3])]
        return jnp.concatenate([jnp.concatenate(pair, 1) for pair in pairs], 0)

    def square(x):
        return jnp.concatenate([jnp.concatenate(x[0:2], 1), jnp.concatenate(x[2:4], 1)], 0)

    def back_four(s, row_buf):
        x = [row_buf[lax.shift_right_logical(spots_ref[s + n], shift)] for n in range(4)]
        out = mm(spread(x), square([blocks[s], blocks[s + 2], blocks[s + 1], blocks[s + 3]]), True)
        for n in range(4):
            bwd[:, s + n, :] = out[32 * n : 32 * n + 32, 128 * (n & 1) : 128 * (n & 1) + 128]

    def ahead_four(s, col_buf):
        x = [col_buf[spots_ref[s + n] & (CB - 1)] for n in range(4)]
        out = mm(spread(x), square([blocks[s + n] for n in range(4)]))
        for n in range(4):
            fwd[:, s + n, :] = out[32 * n : 32 * n + 32, 128 * (n & 1) : 128 * (n & 1) + 128]

    def products(four, buf, low, high):
        def turn(g, carry):
            for u in range(UNROLL):
                four((g * UNROLL + u) * 4, buf)
            return carry

        lax.fori_loop(low // (4 * UNROLL), high // (4 * UNROLL), turn, 0)

    pick_r = in_row_f.astype(BF16)
    pick_c = in_col_f.astype(BF16)

    def gather_sum(pick, terms):
        return mm(pick, terms.astype(BF16))

    def col_part():
        for m in range(32):
            out_c[:, m, :] = gather_sum(pick_c, bwd[m])

        def to_wire(v, carry):
            for p in range(2 * PS):
                out_cb[v * 2 * PS + p] = out_c[v * 2 * PS + p].astype(BF16)
            return carry

        lax.fori_loop(0, C // 2, to_wire, 0)

    def row_part():
        for m in range(32):
            out_r[:, m, :] = gather_sum(pick_r, fwd[m])
        for v in range(RB):
            out_rb[v] = out_r[v].astype(BF16)

    ways = (1, Y - 1) if Y == 4 else (1,)

    def relay_way(kz):
        return 0 if kz % 2 == 0 else 1

    places = [lax.rem(z + kz, Z) for kz in range(Z)]
    order = list(reversed(near_first)) + [0]

    def target(ky, kz):
        return pl.ds((lax.rem(y + ky, Y) * Z + places[kz]) * PS, PS)

    def half(turn, src, kz, w):
        copy(src, yr.at[turn, kz, w], rs_sem.at[turn, 0], rs_y.at[turn, kz], y_dev(ways[w])).start()

    def start_col_sum(turn):
        relays = {}
        if Y == 4:
            for kz in order:
                relays[kz] = copy(
                    out_cb.at[target(2, kz)],
                    relay_in.at[turn, kz],
                    rs_sem.at[turn, 0],
                    rs_relay.at[turn, kz],
                    y_dev(ways[relay_way(kz)]),
                )
                relays[kz].start()
        for kz in order:
            for w, ky in enumerate(ways):
                if Y != 4 or w != relay_way(kz):
                    half(turn, out_cb.at[target(ky, kz)], kz, w)
        return relays

    def start_row_sum(turn):
        for k in range(1, R):
            src = out_rb.at[pl.ds(lax.rem(a + k, R) * PS, PS)]
            copy(src, rr.at[turn, k], rs_sem.at[turn, 3], rs_sem.at[turn, 4], row_dev(k)).start()

    def hand_on(turn, relays):
        for kz in relays:
            w = relay_way(kz)
            relays[kz].wait_recv()
            total = out_c[target(ways[w], kz)] + relay_in[turn, kz].astype(F32)
            relay_out[turn, kz] = total.astype(BF16)
            half(turn, relay_out.at[turn, kz], kz, w)

    def start_z_sum(turn):
        for kz in order:
            total = out_c[target(0, kz)]
            wait_all(yr.at[turn, kz], rs_y.at[turn, kz])
            for w in range(len(ways)):
                total = total + yr[turn, kz, w].astype(F32)
            if kz:
                zs[turn, kz] = total.astype(BF16)
                copy(
                    zs.at[turn, kz], zr.at[turn, kz], rs_sem.at[turn, 1], rs_sem.at[turn, 2], z_dev(kz)
                ).start()
        return total

    def finish_sums(turn, own):
        y_sent, z_sent, z_got, row_sent, row_got = [rs_sem.at[turn, n] for n in range(5)]
        own = own + out_r[pl.ds(a * PS, PS)]
        wait_all(zr.at[turn, pl.ds(1, Z - 1)], z_got)
        for kz in range(1, Z):
            own = own + zr[turn, kz].astype(F32)
        wait_all(rr.at[turn, pl.ds(1, R - 1)], row_got)
        for k in range(1, R):
            own = own + rr[turn, k].astype(F32)
        wait_all(out_cb.at[pl.ds(0, (Y - 1) * Z * PS)], y_sent)
        wait_all(rr.at[turn, pl.ds(1, R - 1)], row_sent)
        wait_all(zr.at[turn, pl.ds(1, Z - 1)], z_sent)
        return own

    class Reduce:
        def __init__(self, turn, buf, buf_in):
            self.turn, self.buf, self.buf_in = turn, buf, buf_in

        def start(self, stage, value):
            count, dev = ((R, row_dev), (Z, z_dev), (Y, y_dev))[stage]
            self.buf[stage] = value
            for k in range(1, count):
                copy(
                    self.buf.at[stage],
                    self.buf_in.at[stage, k],
                    ar_sem.at[self.turn, stage, 0],
                    ar_sem.at[self.turn, stage, 1],
                    dev(k),
                ).start()

        def finish(self, stage):
            count = (R, Z, Y)[stage]
            there = self.buf_in.at[stage, pl.ds(1, count - 1)]
            wait_all(there, ar_sem.at[self.turn, stage, 1])
            total = self.buf[stage]
            for k in range(1, count):
                total = total + self.buf_in[stage, k]
            wait_all(there, ar_sem.at[self.turn, stage, 0])
            return total

    products(back_four, xr, 0, SLOTS)
    col_part()
    relays = start_col_sum(0)
    for n in range(2):
        wait_all(scl_c.at[pl.ds(0, C - 1)], sc_sem.at[n])
    gather1.finish_col()
    lax.fori_loop(0, C, scale_cols, 0)
    products(ahead_four, xc, 0, SLOTS // 2)
    hand_on(0, relays)
    products(ahead_four, xc, SLOTS // 2, SLOTS)
    row_part()
    start_row_sum(0)
    summed = finish_sums(0, start_z_sum(0))
    scaling = scale[...]
    for p in range(PS):
        u1 = (0.5 * WEIGHT) * scaling[p : p + 1] * summed[p]
        basis[32:64, p * 128 : (p + 1) * 128] = u1
        part = (scaling[p : p + 1] * u1).astype(BF16)
        xc2[b * PS + p] = part
        xr2[a * PS + p] = part
    gather2 = Gather(1, xc2, xr2)
    gather2.start()
    early = Reduce(0, gram_e, gram_ei)
    g0 = mm_high(basis[0:64, :], basis[0:64, :], True)
    early.start(
        0, jnp.concatenate([pack(g0[0:32]), pack(g0[0:32, 32:64]), pack(g0[32:64, 32:64])], axis=0)
    )
    gather2.forward(0, 2)
    gather2.finish_row()
    products(back_four, xr2, 0, SLOTS // 4)
    gather2.forward(2, 4)
    products(back_four, xr2, SLOTS // 4, SLOTS // 2)
    gather2.forward(4)
    early.start(1, early.finish(0))
    products(back_four, xr2, SLOTS // 2, SLOTS)
    col_part()
    relays = start_col_sum(1)
    early.start(2, early.finish(1))

    held = {}

    def first_inverses():
        grams = early.finish(2)
        g00 = symmetric(unpack(grams[0:8]))
        g01 = unpack(grams[8:16])
        g11 = symmetric(unpack(grams[16:24]))
        s01 = symmetric(g01)
        inv_curve = inverse(g00 - s01)
        inv_gram = inverse(g00)
        held["all"] = g00, g01, g11, s01, inv_curve, inv_gram

    def first_systems():
        g00, g01, g11, s01, inv_curve, inv_gram = held["all"]
        p1 = small_mm(g00, inv_curve)
        p0 = -small_mm(s01, inv_curve)
        p0_t, p1_t = flip(p0), flip(p1)
        newgram = small_mm(small_mm(p0, g00), p0_t) + small_mm(small_mm(p1, g11), p1_t)
        newgram = symmetric(newgram + 2.0 * small_mm(small_mm(p0, g01), p1_t))
        d0 = p0 + small_mm(newgram, inv_gram)
        direction = lanes(d0[:, 0:32], p1[:, 0:32])
        applied = lanes(d0[:, 0:32], p1[:, 0:32] - d0[:, 0:32], -p1[:, 0:32])
        whole = jnp.concatenate(
            [
                lanes(g00[:, 0:32], g01[:, 0:32], g11[:, 0:32]),
                lanes(flip(g01)[:, 0:32], g11[:, 0:32]),
            ],
            axis=0,
        )
        known = small_mm(direction, mm_high(whole, tall(applied).T))
        coef = jnp.concatenate([direction, lanes(p0[:, 0:32], p1[:, 0:32]), p1], axis=0)
        vectors[...] = mm_high(coef, basis[...])
        return newgram, p1, p1_t, applied, known

    gather2.finish_col()

    def add_share(g, total):
        for n in range(0, 2 * PS, 2):
            v = g * 2 * PS + n
            here = jnp.concatenate([xc2[v], xc2[v + 1]], axis=1)
            there = jnp.concatenate([out_cb[v], out_cb[v + 1]], axis=1)
            total = total + mm(here, there, True)
        return total

    share = lax.fori_loop(0, C // 2, add_share, jnp.zeros((32, 32), F32))
    late = Reduce(1, gram_l, gram_li)
    late.start(0, pack(WEIGHT * share))
    products(ahead_four, xc2, 0, SLOTS // 2)
    hand_on(1, relays)
    late.start(1, late.finish(0))
    products(ahead_four, xc2, SLOTS // 2, SLOTS)
    late.start(2, late.finish(1))
    first_inverses()
    row_part()
    start_row_sum(1)
    own = start_z_sum(1)
    newgram, p1, p1_t, applied, known = first_systems()
    g12 = symmetric(unpack(late.finish(2)))
    curve = symmetric(known - small_mm(small_mm(p1, g12), p1_t))
    steps = small_mm(newgram, inverse(curve))
    sol_ref[...] = vectors[64:96, :] + mm_high(steps, tall(vectors[0:32, :]))
    summed = finish_sums(1, own)
    scaling = scale[...]
    for p in range(PS):
        u2 = (0.5 * WEIGHT) * scaling[p : p + 1] * summed[p]
        basis[64:96, p * 128 : (p + 1) * 128] = u2
    image = mm_high(applied, basis[...])
    res_ref[...] = vectors[32:64, :] - mm_high(steps, tall(image))


def split_col(count):
    return (4, count // 4) if count >= 8 else (2, count // 2)


def solution(mesh):
    R, C = mesh.shape["row"], mesh.shape["col"]
    Y, Z = split_col(C)
    RB, CB = R * PS, C * PS

    def body(queries, block_spots, live_blocks, neighbor_cols, neighbor_sims):
        slots = block_spots.shape[2]
        vmem = pltpu.VMEM
        sems = pltpu.SemaphoreType.DMA
        ways = 2 if Y == 4 else 1
        scratch = [
            vmem(queries.shape, F32), vmem((1, slots), jnp.int32),
            vmem(neighbor_cols.shape[2:], jnp.int32), vmem(neighbor_sims.shape[2:], BF16),
            vmem((slots, 128, 128), BF16), vmem((slots, 128), F32), vmem((slots, 128), F32),
            vmem((128, PS * 128), F32), vmem((96, PS * 128), F32), vmem((PS, 128), F32),
            vmem((CB, 32, 128), BF16), vmem((RB, 32, 128), BF16),
            vmem((CB, 32, 128), BF16), vmem((RB, 32, 128), BF16),
            vmem((32, slots, 128), F32), vmem((32, slots, 128), F32),
            vmem((RB, 32, 128), F32), vmem((CB, 32, 128), F32),
            vmem((RB, 32, 128), BF16), vmem((CB, 32, 128), BF16),
            vmem((R, PS, 128), F32), vmem((C, PS, 128), F32),
            vmem((R, PS, 128), F32), vmem((C, PS, 128), F32),
            vmem((R, PS, 128), F32), vmem((C, PS, 128), F32),
            vmem((2, Z, ways, PS, 32, 128), BF16), vmem((2, Z, PS, 32, 128), BF16),
            vmem((2, Z, PS, 32, 128), BF16), vmem((2, Z, PS, 32, 128), BF16),
            vmem((2, Z, PS, 32, 128), BF16), vmem((2, R, PS, 32, 128), BF16),
            vmem((3, 24, 128), F32), vmem((3, max(R, Z, Y), 24, 128), F32),
            vmem((3, 8, 128), F32), vmem((3, max(R, Z, Y), 8, 128), F32),
            sems((10,)), sems((2, Z)), sems((2, 4)), sems((4,)), sems((4,)),
            sems((2, Z)), sems((2, Z)), sems((2, 5)), sems((2, 3, 2)),
        ]
        in_vmem = pl.BlockSpec(memory_space=pltpu.VMEM)
        in_any = pl.BlockSpec(memory_space=pl.ANY)
        in_smem = pl.BlockSpec(memory_space=pltpu.SMEM)
        shape = jax.ShapeDtypeStruct(queries.shape, F32)
        return pl.pallas_call(
            functools.partial(kernel, (R, Y, Z)),
            out_shape=(shape, shape),
            in_specs=[in_any, in_smem, in_any, in_smem, in_any, in_any],
            out_specs=(in_vmem, in_vmem),
            scratch_shapes=scratch,
            compiler_params=pltpu.CompilerParams(
                collective_id=0, has_side_effects=True, vmem_limit_bytes=53 * 1024 * 1024 + 512 * 1024
            ),
        )(
            queries,
            block_spots[0, 0],
            block_spots[0],
            live_blocks,
            neighbor_cols[0, 0],
            neighbor_sims[0, 0],
        )

    placed = (
        P(None, ("row", "col")),
        P("row", "col", None),
        P("row", "col"),
        P("row", "col", None, None, None),
        P("row", "col", None, None, None),
    )
    return jax.shard_map(
        body,
        mesh=mesh,
        in_specs=placed,
        out_specs=(P(None, ("row", "col")), P(None, ("row", "col"))),
        check_vma=False,
    )
```
